32 devices in a mesh: row: 16 (over z, y, x), col: 2 (over core).
Axes of the slice: x: 2, y: 2, z: 4, core: 2. Of those that a mesh axis runs over, the one named last changes fastest.
Arguments:
- frames: bfloat16 [4, 4096, 2048], P(None, 'row', 'col'), may hold values from -6 to 6
- row_factor: bfloat16 [4096, 256], P('row')
- col_factor: bfloat16 [2048, 256], P('col')
- row_history: float32 [4096, 256], P('row'), may hold values from -8 to 8
- col_history: float32 [2048, 256], P('col'), may hold values from -8 to 8
- time_gram: float32 [256, 256], replicated, as said below
Outputs:
- frame_factor: float32 [4, 256], replicated
- new_row_factor: bfloat16 [4096, 256], P('row')
- new_col_factor: bfloat16 [2048, 256], P('col')
The draws below stay inside these ranges and needn't reach their ends.
Inputs may be any that keep to these rules, and one draw needn't show every extreme that they name: `time_gram`: symmetric positive definite.
All inputs are finite; a program needn't handle non-finite values.
Results may differ from the reference program's by a relative error of at most 0.0041.
Values may be sent and summed in bfloat16 or wider, within the bound.
A program may use at most 64 MiB of HBM per device.

```python
import math
import jax
import jax.numpy as jnp
from jax import lax

R = 256
NB = 4
ROWS = 4096
COLS = 2048


def factor_draw(key, count):
    key_noise, key_common = jax.random.split(key, 2)
    noise = jnp.clip(jax.random.normal(key_noise, (count, R), jnp.float32), -5.0, 5.0)
    common = jnp.clip(jax.random.normal(key_common, (count, 1), jnp.float32), -5.0, 5.0)
    return (noise + 0.7 * common) / math.sqrt(count)


def draw_row_factor(key, part):
    return factor_draw(jax.random.fold_in(key, 11), ROWS).astype(jnp.bfloat16)


def draw_col_factor(key, part):
    return factor_draw(jax.random.fold_in(key, 23), COLS).astype(jnp.bfloat16)


def draw_time_gram(key, part):
    key_off, key_diag = jax.random.split(jax.random.fold_in(key, 37))
    offdiag = jax.random.uniform(key_off, (R, R), jnp.float32, -0.01, 0.01)
    offdiag = 0.5 * (offdiag + offdiag.T)
    diag_vals = jax.random.uniform(key_diag, (R,), jnp.float32, 3.0, 4.0)
    identity = jnp.eye(R, dtype=jnp.float32)
    return offdiag * (1.0 - identity) + identity * diag_vals[None, :]


def steps_of(stream_key, extent, shards, low, high):
    def one(dim, parts):
        steps = jax.random.uniform(jax.random.fold_in(jax.random.fold_in(stream_key, 6), dim), (parts,), jnp.float32, low / len(shards), high / len(shards))
        return jnp.repeat(jnp.exp(steps), extent[dim] // parts).reshape((-1,) + (1,) * (len(extent) - dim - 1))

    loudness = one(*shards[0])
    for cut in shards[1:]:
        loudness = loudness * one(*cut)
    return loudness


def gaussian(stream_key, dims, spread, limit, cuts=(), kind=jnp.bfloat16):
    result = spread * jax.random.normal(stream_key, dims, jnp.float32)
    if cuts:
        result = result * steps_of(stream_key, dims, cuts, -0.22, 0.18)
    return jnp.clip(result, -limit, limit).astype(kind)


def setup_inputs(seed: int = 0) -> dict:
    key_list = jax.random.split(jax.random.key(seed), 7)
    frames = gaussian(key_list[0], (NB, ROWS, COLS), 1.0, 6.0, ((1, 16), (2, 2)))
    row_factor = draw_row_factor(jax.random.fold_in(key_list[6], 71), 0)
    col_factor = draw_col_factor(jax.random.fold_in(key_list[6], 71), 0)
    row_history = gaussian(key_list[3], (ROWS, R), 2.0, 8.0, ((0, 16),), jnp.float32)
    col_history = gaussian(key_list[4], (COLS, R), 2.0, 8.0, ((0, 2),), jnp.float32)
    time_gram = draw_time_gram(jax.random.fold_in(key_list[6], 71), 0)
    return {"frames": frames, "row_factor": row_factor, "col_factor": col_factor, "row_history": row_history, "col_history": col_history, "time_gram": time_gram}


def inner_gram(matrix):
    return lax.dot_general(matrix.astype(jnp.float32), matrix.astype(jnp.float32), (((0,), (0,)), ((), ())), preferred_element_type=jnp.float32)

def gram_solve(rhs, gram):
    lower_factor = jnp.linalg.cholesky(gram)
    return jax.scipy.linalg.cho_solve((lower_factor, True), rhs.T).T

def reference(frames, row_factor, col_factor, row_history, col_history, time_gram):
    row_gram = inner_gram(row_factor)
    col_gram = inner_gram(col_factor)

    def slab_one(frame):
        return jnp.dot(frame.astype(jnp.float32), col_factor.astype(jnp.float32), preferred_element_type=jnp.float32)
    slab_products = lax.map(slab_one, frames)
    frame_rhs = jnp.sum(slab_products * row_factor.astype(jnp.float32)[None], axis=1)
    frame_factor = gram_solve(frame_rhs, row_gram * col_gram)
    time_new = time_gram + jnp.dot(frame_factor.T, frame_factor, precision=lax.Precision.HIGHEST)
    row_sums = row_history + jnp.sum(frame_factor[:, None, :] * slab_products, axis=0)
    new_row = gram_solve(row_sums, time_new * col_gram).astype(jnp.bfloat16)
    new_row_gram = inner_gram(new_row)

    def column_one(frame):
        return lax.dot_general(frame.astype(jnp.float32), new_row.astype(jnp.float32), (((0,), (0,)), ((), ())), preferred_element_type=jnp.float32)
    col_prods = lax.map(column_one, frames)
    col_sums = col_history + jnp.sum(frame_factor[:, None, :] * col_prods, axis=0)
    new_col = gram_solve(col_sums, time_new * new_row_gram).astype(jnp.bfloat16)
    return (frame_factor, new_row, new_col)
```

```python
import functools

import jax
import jax.numpy as jnp
from jax import lax
from jax.experimental import pallas as pl
from jax.experimental.pallas import tpu as pltpu
from jax.sharding import PartitionSpec as P

MESH = pl.DeviceIdType.MESH
HIGHEST = lax.Precision.HIGHEST
F32 = jnp.float32
PIV = 4


def dot(a, b, dims, precision=None):
    return lax.dot_general(a, b, (dims, ((), ())), precision=precision, preferred_element_type=F32)


def small_inverse(m):
    m = [list(row) for row in m]
    size = len(m)
    for k in range(size):
        p = 1.0 / m[k][k]
        row = [p if j == k else m[k][j] * p for j in range(size)]
        for i in range(size):
            if i != k:
                f = m[i][k]
                m[i] = [-(f * p) if j == k else m[i][j] - f * row[j] for j in range(size)]
        m[k] = row
    return m


def invert(a_ref):
    n = a_ref.shape[0]
    lane = lax.broadcasted_iota(jnp.int32, (1, n), 1)
    step = 64

    def group(g, carry):
        base = pl.multiple_of(g * 8, 8)
        for j in range(0, 8, PIV):
            last = j + PIV == 8
            tile = a_ref[pl.ds(base, 8), :]
            m = [[tile[j + a : j + a + 1, j + b : j + b + 1] for b in range(PIV)] for a in range(PIV)]
            mi = small_inverse(m)
            inside = (lane >= j) & (lane < j + PIV)
            rows = [
                jnp.where(lane == j + b, 1.0, jnp.where(inside, 0.0, tile[j + b : j + b + 1, :]))
                for b in range(PIV)
            ]
            w = [sum(mi[a][b] * rows[b] for b in range(PIV)) for a in range(PIV)]
            for r in range(0, n, step):
                x = a_ref[r : r + step, :]
                y = jnp.where(inside, 0.0, x)
                for a in range(PIV):
                    y = y - x[:, j + a : j + a + 1] * w[a]
                a_ref[r : r + step, :] = pltpu.roll(y, n - 8, 1) if last else y
            for a in range(PIV):
                a_ref[pl.ds(base + j + a, 1), :] = pltpu.roll(w[a], n - 8, 1) if last else w[a]
        return carry

    lax.fori_loop(0, n // 8, group, 0)


def kernel(nrow, ncol, frames, rf, cf, rhist, chist, tgram, o_f, o_row, o_col,
           slab, cgram, rpart, rrecv, rfull, rhs, gpart, grecv, gfull, ppart, precv, pfull,
           mat, tnew, total,
           slab_s, slab_r, cg_s, cg_r, rs_s, rs_r, ag_s, ag_r, rhs_s, rhs_r,
           gs_s, gs_r, ga_s, ga_r, ps_s, ps_r, pa_s, pa_r):
    row = lax.axis_index("row")
    col = lax.axis_index("col")
    nb = frames.shape[0]
    rank = rf.shape[1]
    ch = rank // nrow
    pch = cf.shape[0] // nrow

    def send_all(axis, me, count, src, dst, s_sem, r_sem):
        def one(d, carry):
            p = lax.rem(me + d, count)
            pltpu.make_async_remote_copy(
                src_ref=src(p), dst_ref=dst, send_sem=s_sem.at[p], recv_sem=r_sem.at[me],
                device_id={axis: p}, device_id_type=MESH,
            ).start()
            return carry
        lax.fori_loop(1, count, one, 0)

    def wait_all(axis, me, count, src, dst, s_sem, r_sem, recv):
        def one(d, carry):
            p = lax.rem(me + d, count)
            copy = pltpu.make_async_remote_copy(
                src_ref=src(p), dst_ref=dst(p), send_sem=s_sem.at[p], recv_sem=r_sem.at[p],
                device_id={axis: p}, device_id_type=MESH,
            )
            if recv:
                copy.wait_recv()
            else:
                copy.wait_send()
            return carry
        lax.fori_loop(1, count, one, 0)

    exchanges = {
        "slab": ("col", col, ncol, lambda p: slab.at[col], slab, slab_s, slab_r),
        "cgram": ("col", col, ncol, lambda p: cgram.at[col], cgram, cg_s, cg_r),
        "rs": ("row", row, nrow, lambda p: rpart.at[p], rrecv, rs_s, rs_r),
        "ag": ("row", row, nrow, lambda p: rfull.at[row], rfull, ag_s, ag_r),
        "rhs": ("row", row, nrow, lambda p: rhs.at[row], rhs, rhs_s, rhs_r),
        "gs": ("row", row, nrow, lambda p: gpart.at[p], grecv, gs_s, gs_r),
        "ga": ("row", row, nrow, lambda p: gfull.at[row], gfull, ga_s, ga_r),
        "ps": ("row", row, nrow, lambda p: ppart.at[p], precv, ps_s, ps_r),
        "pa": ("row", row, nrow, lambda p: pfull.at[row], pfull, pa_s, pa_r),
    }

    def send(name):
        axis, me, count, src, buf, s, r = exchanges[name]
        send_all(axis, me, count, src, buf.at[me], s, r)

    def wait(name, recv=True):
        axis, me, count, src, buf, s, r = exchanges[name]
        wait_all(axis, me, count, src, lambda p: buf.at[p], s, r, recv)

    barrier = pltpu.get_barrier_semaphore()

    def greet(axis, me, count):
        def one(d, carry):
            pl.semaphore_signal(
                barrier, inc=1, device_id={axis: lax.rem(me + d, count)}, device_id_type=MESH
            )
            return carry
        lax.fori_loop(1, count, one, 0)

    greet("row", row, nrow)
    greet("col", col, ncol)

    gram = dot(rf[...], rf[...], ((0,), (0,)))
    for i in range(nrow):
        rpart[i] = gram[i * ch : (i + 1) * ch]
    rrecv[row] = rpart[row]
    cgram[col] = dot(cf[...], cf[...], ((0,), (0,)))
    pl.semaphore_wait(barrier, nrow + ncol - 2)
    send("rs")
    send("cgram")

    def slab_one(b, carry):
        slab[col, b] = dot(frames[b], cf[...], ((1,), (0,)))
        return carry

    lax.fori_loop(0, nb, slab_one, 0)
    send("slab")

    wait("rs")
    rfull[row] = sum((rrecv[i] for i in range(1, nrow)), rrecv[0])
    send("ag")

    wait("slab")
    for b in range(nb):
        s = sum((slab[c, b] for c in range(1, ncol)), slab[0, b])
        total[b] = s
        rhs[row, b : b + 1, :] = jnp.sum(s * rf[...].astype(F32), axis=0, keepdims=True)
    rhs[row, nb:8, :] = jnp.zeros((8 - nb, rank), F32)
    send("rhs")

    wait("cgram")
    tnew[...] = sum((cgram[c] for c in range(1, ncol)), cgram[0])
    wait("ag")
    for i in range(nrow):
        mat[i * ch : (i + 1) * ch, :] = rfull[i] * tnew[i * ch : (i + 1) * ch, :]
    invert(mat)
    wait("rhs")
    right = sum((rhs[i] for i in range(1, nrow)), rhs[0])
    ff = dot(right, mat[...], ((1,), (0,)), HIGHEST)
    o_f[...] = ff[:nb]

    time_new = tgram[...] + dot(ff, ff, ((0,), (0,)), HIGHEST)
    mat[...] = time_new * tnew[...]
    tnew[...] = time_new
    invert(mat)
    sums = rhist[...]
    for b in range(nb):
        sums = sums + ff[b : b + 1, :] * total[b]
    new_row = dot(sums, mat[...], ((1,), (0,)), HIGHEST).astype(jnp.bfloat16)
    o_row[...] = new_row

    gram = dot(new_row, new_row, ((0,), (0,)))
    for i in range(nrow):
        gpart[i] = gram[i * ch : (i + 1) * ch]
    grecv[row] = gpart[row]
    send("gs")
    wide = 256
    for j in range(0, cf.shape[0], wide):
        acc = jnp.zeros((wide, rank), F32)
        for b in range(nb):
            acc = acc + ff[b : b + 1, :] * dot(
                frames[b, :, j : j + wide], new_row, ((0,), (0,))
            )
        acc = acc.astype(jnp.bfloat16)
        for i in range(wide // pch):
            ppart[j // pch + i] = acc[i * pch : (i + 1) * pch]
    wait("gs")
    gfull[row] = sum((grecv[i] for i in range(1, nrow)), grecv[0])
    send("ga")
    precv[row] = ppart[row]
    send("ps")
    wait("ga")
    for i in range(nrow):
        mat[i * ch : (i + 1) * ch, :] = gfull[i] * tnew[i * ch : (i + 1) * ch, :]
    invert(mat)
    wait("ps")
    own = chist[pl.ds(pl.multiple_of(row * pch, pch), pch), :]
    for i in range(nrow):
        own = own + precv[i].astype(F32)
    pfull[row] = dot(own, mat[...], ((1,), (0,)), HIGHEST).astype(jnp.bfloat16)
    send("pa")
    wait("pa")
    for i in range(nrow):
        o_col[i * pch : (i + 1) * pch, :] = pfull[i]

    for name in exchanges:
        wait(name, recv=False)


def body(nrow, ncol, frames, rf, cf, rhist, chist, tgram):
    nb, rows, cols = frames.shape
    rank = rf.shape[1]
    ch, pch = rank // nrow, cols // nrow
    vm = pltpu.VMEM
    bf = jnp.bfloat16
    dma = pltpu.SemaphoreType.DMA
    counts = [ncol, ncol] + [nrow] * 7
    sems = [dma((c,)) for c in counts for _ in range(2)]
    space = pl.BlockSpec(memory_space=vm)
    flops = 2 * (2 * nb * rows * cols * rank + cols * rank * rank + 8 * rank**3)
    return pl.pallas_call(
        functools.partial(kernel, nrow, ncol),
        out_shape=(
            jax.ShapeDtypeStruct((nb, rank), F32),
            jax.ShapeDtypeStruct((rows, rank), bf),
            jax.ShapeDtypeStruct((cols, rank), bf),
        ),
        in_specs=[space] * 6,
        out_specs=(space,) * 3,
        scratch_shapes=[
            vm((ncol, nb, rows, rank), F32),
            vm((ncol, rank, rank), F32),
            vm((nrow, ch, rank), F32),
            vm((nrow, ch, rank), F32),
            vm((nrow, ch, rank), F32),
            vm((nrow, 8, rank), F32),
            vm((nrow, ch, rank), F32),
            vm((nrow, ch, rank), F32),
            vm((nrow, ch, rank), F32),
            vm((nrow, pch, rank), bf),
            vm((nrow, pch, rank), bf),
            vm((nrow, pch, rank), bf),
            vm((rank, rank), F32),
            vm((rank, rank), F32),
            vm((nb, rows, rank), F32),
        ] + sems,
        compiler_params=pltpu.CompilerParams(
            collective_id=0, has_side_effects=True, vmem_limit_bytes=48 * 1024 * 1024
        ),
        cost_estimate=pl.CostEstimate(
            flops=flops, bytes_accessed=frames.size * 2 + 4 * cols * rank * 2, transcendentals=0
        ),
    )(frames, rf, cf, rhist, chist, tgram)


def solution(mesh):
    in_specs = (
        P(None, "row", "col"),
        P("row", None),
        P("col", None),
        P("row", None),
        P("col", None),
        P(),
    )
    out_specs = (P(), P("row", None), P("col", None))
    return jax.shard_map(
        functools.partial(body, mesh.shape["row"], mesh.shape["col"]),
        mesh=mesh, in_specs=in_specs, out_specs=out_specs, check_vma=False,
    )
```

```python
import functools

import jax
import jax.numpy as jnp
from jax import lax
from jax.experimental import pallas as pl
from jax.experimental.pallas import tpu as pltpu
from jax.sharding import PartitionSpec as P

MESH = pl.DeviceIdType.MESH
HIGHEST = lax.Precision.HIGHEST
F32 = jnp.float32
PIV = 8


def dot(a, b, dims, precision=None):
    return lax.dot_general(a, b, (dims, ((), ())), precision=precision, preferred_element_type=F32)


def eliminate(tile, lane):
    n = tile.shape[1]
    wide = (PIV, 128)
    sub = lax.broadcasted_iota(jnp.int32, wide, 0)
    cols = [jnp.broadcast_to(tile[:, b : b + 1], wide) for b in range(PIV)]
    for k in range(PIV):
        row = [jnp.broadcast_to(c[k : k + 1, :], wide) for c in cols]
        p = 1.0 / row[k]
        ck = cols[k]
        here = sub == k
        for b in range(PIV):
            if b == k:
                cols[b] = jnp.where(here, p, -(ck * p))
            else:
                w = row[b] * p
                cols[b] = jnp.where(here, w, cols[b] - ck * w)
    unit = (lane == lax.broadcasted_iota(jnp.int32, (PIV, n), 0)).astype(F32)
    tile = jnp.where(lane < PIV, unit, tile)
    out = None
    for b in range(PIV):
        scale = jnp.concatenate([cols[b]] * (n // 128), axis=1)
        term = scale * jnp.broadcast_to(tile[b : b + 1, :], (PIV, n))
        out = term if out is None else out + term
    return out


def spread(w):
    return [jnp.broadcast_to(w[a : a + 1, :], w.shape) for a in range(PIV)]


def update(x, ws, lane):
    y = jnp.where(lane < PIV, 0.0, x)
    for a in range(PIV):
        y = y - jnp.broadcast_to(x[:, a : a + 1], x.shape) * ws[a]
    return pltpu.roll(y, x.shape[1] - PIV, 1)


def invert(a_ref):
    n = a_ref.shape[0]
    groups = n // PIV
    lane = lax.broadcasted_iota(jnp.int32, (PIV, n), 1)

    def rows(g):
        return pl.ds(pl.multiple_of(g * PIV, PIV), PIV)

    def bulk(g, w, ws):
        for r in range(0, n, PIV):
            a_ref[r : r + PIV, :] = update(a_ref[r : r + PIV, :], ws, lane)
        a_ref[rows(g), :] = pltpu.roll(w, n - PIV, 1)

    w = eliminate(a_ref[0:PIV, :], lane)
    tile = update(a_ref[PIV : 2 * PIV, :], spread(w), lane)

    def group(g, carry):
        w, tile = carry
        ws = spread(w)
        later = update(a_ref[rows(lax.rem(g + 1, groups)), :], ws, lane)
        fresh = eliminate(tile, lane)
        bulk(g - 1, w, ws)
        return fresh, update(later, spread(fresh), lane)

    w, _ = lax.fori_loop(1, groups, group, (w, tile))
    bulk(groups - 1, w, spread(w))


def kernel(nrow, ncol, frames_h, rf_h, cf_h, rhist_h, chist_h, tgram_h, o_f, o_row, o_col,
           frames, rf, cf, rhist, chist, tgram, in_s, slab, cgram, rpart, rrecv, rfull, rhs, gpart, grecv, gfull, ppart, precv, pfull,
           mat, tnew, total,
           slab_s, slab_r, cg_s, cg_r, rs_s, rs_r, ag_s, ag_r, rhs_s, rhs_r,
           gs_s, gs_r, ga_s, ga_r, ps_s, ps_r, pa_s, pa_r):
    row = lax.axis_index("row")
    col = lax.axis_index("col")
    nb = frames.shape[0]
    rank = rf.shape[1]
    ch = rank // nrow
    pch = cf.shape[0] // nrow

    def send_all(axis, me, count, src, dst, s_sem, r_sem):
        def one(d, carry):
            p = lax.rem(me + d, count)
            pltpu.make_async_remote_copy(
                src_ref=src(p), dst_ref=dst, send_sem=s_sem.at[p], recv_sem=r_sem.at[me],
                device_id={axis: p}, device_id_type=MESH,
            ).start()
            return carry
        lax.fori_loop(1, count, one, 0)

    def wait_all(axis, me, count, src, dst, s_sem, r_sem, recv):
        def one(d, carry):
            p = lax.rem(me + d, count)
            copy = pltpu.make_async_remote_copy(
                src_ref=src(p), dst_ref=dst(p), send_sem=s_sem.at[p], recv_sem=r_sem.at[p],
                device_id={axis: p}, device_id_type=MESH,
            )
            if recv:
                copy.wait_recv()
            else:
                copy.wait_send()
            return carry
        lax.fori_loop(1, count, one, 0)

    exchanges = {
        "slab": ("col", col, ncol, lambda p: slab.at[col], slab, slab_s, slab_r),
        "cgram": ("col", col, ncol, lambda p: cgram.at[col], cgram, cg_s, cg_r),
        "rs": ("row", row, nrow, lambda p: rpart.at[p], rrecv, rs_s, rs_r),
        "ag": ("row", row, nrow, lambda p: rfull.at[row], rfull, ag_s, ag_r),
        "rhs": ("row", row, nrow, lambda p: rhs.at[row], rhs, rhs_s, rhs_r),
        "gs": ("row", row, nrow, lambda p: gpart.at[p], grecv, gs_s, gs_r),
        "ga": ("row", row, nrow, lambda p: gfull.at[row], gfull, ga_s, ga_r),
        "ps": ("row", row, nrow, lambda p: ppart.at[p], precv, ps_s, ps_r),
        "pa": ("row", row, nrow, lambda p: pfull.at[row], pfull, pa_s, pa_r),
    }

    def send(name):
        axis, me, count, src, buf, s, r = exchanges[name]
        send_all(axis, me, count, src, buf.at[me], s, r)

    def wait(name, recv=True):
        axis, me, count, src, buf, s, r = exchanges[name]
        wait_all(axis, me, count, src, lambda p: buf.at[p], s, r, recv)

    barrier = pltpu.get_barrier_semaphore()

    def greet(axis, me, count):
        def one(d, carry):
            pl.semaphore_signal(
                barrier, inc=1, device_id={axis: lax.rem(me + d, count)}, device_id_type=MESH
            )
            return carry
        lax.fori_loop(1, count, one, 0)

    loads = [
        pltpu.make_async_copy(src, dst, in_s.at[i])
        for i, (src, dst) in enumerate(
            [(rf_h, rf), (cf_h, cf), (frames_h, frames), (tgram_h, tgram), (rhist_h, rhist), (chist_h, chist)]
        )
    ]
    for load in loads:
        load.start()
    greet("row", row, nrow)
    greet("col", col, ncol)
    loads[0].wait()

    gram = dot(rf[...], rf[...], ((0,), (0,)))
    for i in range(nrow):
        rpart[i] = gram[i * ch : (i + 1) * ch]
    rrecv[row] = rpart[row]
    loads[1].wait()
    cgram[col] = dot(cf[...], cf[...], ((0,), (0,)))
    pl.semaphore_wait(barrier, nrow + ncol - 2)
    send("rs")
    send("cgram")

    def slab_one(b, carry):
        slab[col, b] = dot(frames[b], cf[...], ((1,), (0,)))
        return carry

    loads[2].wait()
    lax.fori_loop(0, nb, slab_one, 0)
    send("slab")

    wait("rs")
    rfull[row] = sum((rrecv[i] for i in range(1, nrow)), rrecv[0])
    send("ag")

    wait("slab")
    for b in range(nb):
        s = sum((slab[c, b] for c in range(1, ncol)), slab[0, b])
        total[b] = s
        rhs[row, b : b + 1, :] = jnp.sum(s * rf[...].astype(F32), axis=0, keepdims=True)
    rhs[row, nb:8, :] = jnp.zeros((8 - nb, rank), F32)
    send("rhs")

    wait("cgram")
    tnew[...] = sum((cgram[c] for c in range(1, ncol)), cgram[0])
    wait("ag")
    for i in range(nrow):
        mat[i * ch : (i + 1) * ch, :] = rfull[i] * tnew[i * ch : (i + 1) * ch, :]
    invert(mat)
    wait("rhs")
    right = sum((rhs[i] for i in range(1, nrow)), rhs[0])
    ff = dot(right, mat[...], ((1,), (0,)), HIGHEST)
    o_f[...] = ff[:nb]

    for load in loads[3:]:
        load.wait()
    time_new = tgram[...] + dot(ff, ff, ((0,), (0,)), HIGHEST)
    mat[...] = time_new * tnew[...]
    tnew[...] = time_new
    invert(mat)
    sums = rhist[...]
    for b in range(nb):
        sums = sums + ff[b : b + 1, :] * total[b]
    new_row = dot(sums, mat[...], ((1,), (0,)), HIGHEST).astype(jnp.bfloat16)
    o_row[...] = new_row

    gram = dot(new_row, new_row, ((0,), (0,)))
    for i in range(nrow):
        gpart[i] = gram[i * ch : (i + 1) * ch]
    grecv[row] = gpart[row]
    send("gs")
    wide = 256
    for j in range(0, cf.shape[0], wide):
        acc = jnp.zeros((wide, rank), F32)
        for b in range(nb):
            acc = acc + ff[b : b + 1, :] * dot(
                frames[b, :, j : j + wide], new_row, ((0,), (0,))
            )
        acc = acc.astype(jnp.bfloat16)
        for i in range(wide // pch):
            ppart[j // pch + i] = acc[i * pch : (i + 1) * pch]
    wait("gs")
    gfull[row] = sum((grecv[i] for i in range(1, nrow)), grecv[0])
    send("ga")
    precv[row] = ppart[row]
    send("ps")
    wait("ga")
    for i in range(nrow):
        mat[i * ch : (i + 1) * ch, :] = gfull[i] * tnew[i * ch : (i + 1) * ch, :]
    invert(mat)
    wait("ps")
    own = chist[pl.ds(pl.multiple_of(row * pch, pch), pch), :]
    for i in range(nrow):
        own = own + precv[i].astype(F32)
    pfull[row] = dot(own, mat[...], ((1,), (0,)), HIGHEST).astype(jnp.bfloat16)
    send("pa")
    wait("pa")
    for i in range(nrow):
        o_col[i * pch : (i + 1) * pch, :] = pfull[i]

    for name in exchanges:
        wait(name, recv=False)


def body(nrow, ncol, frames, rf, cf, rhist, chist, tgram):
    nb, rows, cols = frames.shape
    rank = rf.shape[1]
    ch, pch = rank // nrow, cols // nrow
    vm = pltpu.VMEM
    bf = jnp.bfloat16
    dma = pltpu.SemaphoreType.DMA
    counts = [ncol, ncol] + [nrow] * 7
    sems = [dma((c,)) for c in counts for _ in range(2)]
    space = pl.BlockSpec(memory_space=vm)
    flops = 2 * (2 * nb * rows * cols * rank + cols * rank * rank + 8 * rank**3)
    return pl.pallas_call(
        functools.partial(kernel, nrow, ncol),
        out_shape=(
            jax.ShapeDtypeStruct((nb, rank), F32),
            jax.ShapeDtypeStruct((rows, rank), bf),
            jax.ShapeDtypeStruct((cols, rank), bf),
        ),
        in_specs=[pl.BlockSpec(memory_space=pltpu.HBM)] * 6,
        out_specs=(space,) * 3,
        scratch_shapes=[vm(x.shape, x.dtype) for x in (frames, rf, cf, rhist, chist, tgram)] + [
            dma((6,)),
            vm((ncol, nb, rows, rank), F32),
            vm((ncol, rank, rank), F32),
            vm((nrow, ch, rank), F32),
            vm((nrow, ch, rank), F32),
            vm((nrow, ch, rank), F32),
            vm((nrow, 8, rank), F32),
            vm((nrow, ch, rank), F32),
            vm((nrow, ch, rank), F32),
            vm((nrow, ch, rank), F32),
            vm((nrow, pch, rank), bf),
            vm((nrow, pch, rank), bf),
            vm((nrow, pch, rank), bf),
            vm((rank, rank), F32),
            vm((rank, rank), F32),
            vm((nb, rows, rank), F32),
        ] + sems,
        compiler_params=pltpu.CompilerParams(
            collective_id=0, has_side_effects=True, vmem_limit_bytes=48 * 1024 * 1024
        ),
        cost_estimate=pl.CostEstimate(
            flops=flops, bytes_accessed=frames.size * 2 + 4 * cols * rank * 2, transcendentals=0
        ),
    )(frames, rf, cf, rhist, chist, tgram)


def solution(mesh):
    in_specs = (
        P(None, "row", "col"),
        P("row", None),
        P("col", None),
        P("row", None),
        P("col", None),
        P(),
    )
    out_specs = (P(), P("row", None), P("col", None))
    return jax.shard_map(
        functools.partial(body, mesh.shape["row"], mesh.shape["col"]),
        mesh=mesh, in_specs=in_specs, out_specs=out_specs, check_vma=False,
    )
```

```python
import functools

import jax
import jax.numpy as jnp
from jax import lax
from jax.experimental import pallas as pl
from jax.experimental.pallas import tpu as pltpu
from jax.sharding import PartitionSpec as P

MESH = pl.DeviceIdType.MESH
HIGHEST = lax.Precision.HIGHEST
F32 = jnp.float32
PIV = 8


def dot(a, b, dims, precision=None):
    return lax.dot_general(a, b, (dims, ((), ())), precision=precision, preferred_element_type=F32)


def eliminate(tile, turned, g, lane):
    n = tile.shape[1]
    wide = (PIV, 128)
    sub = lax.broadcasted_iota(jnp.int32, wide, 0)
    cols = [jnp.broadcast_to(turned[:, b : b + 1], wide) for b in range(PIV)]
    for k in range(PIV):
        row = [jnp.broadcast_to(c[k : k + 1, :], wide) for c in cols]
        p = 1.0 / row[k]
        ck = cols[k]
        here = sub == k
        for b in range(PIV):
            if b == k:
                cols[b] = jnp.where(here, p, -(ck * p))
            else:
                w = row[b] * p
                cols[b] = jnp.where(here, w, cols[b] - ck * w)
    at = lane - g * PIV
    unit = (at == lax.broadcasted_iota(jnp.int32, (PIV, n), 0)).astype(F32)
    tile = jnp.where((at >= 0) & (at < PIV), unit, tile)
    out = None
    for b in range(PIV):
        scale = jnp.concatenate([cols[b]] * (n // 128), axis=1)
        term = scale * jnp.broadcast_to(tile[b : b + 1, :], (PIV, n))
        out = term if out is None else out + term
    return out


def invert(a_ref, w_ref):
    n = a_ref.shape[0]
    groups = n // PIV
    lane = lax.broadcasted_iota(jnp.int32, (PIV, n), 1)
    lanes = lax.broadcasted_iota(jnp.int32, (n, n), 1)

    def rows(g):
        return pl.ds(pl.multiple_of(g * PIV, PIV), PIV)

    def front(tile, g):
        return pltpu.roll(tile, lax.rem(n - g * PIV, n), 1)

    def update(tile, w, g):
        turned = front(tile, g)
        y = jnp.where((lane >= g * PIV) & (lane < g * PIV + PIV), 0.0, tile)
        for a in range(PIV):
            y = y - jnp.broadcast_to(turned[:, a : a + 1], y.shape) * jnp.broadcast_to(w[a : a + 1, :], y.shape)
        return y

    def bulk(g, w):
        w_ref[rows(g), :] = w
        inside = (lanes >= g * PIV) & (lanes < g * PIV + PIV)
        x = a_ref[...]
        w_all = w_ref[...]
        a_ref[...] = jnp.where(inside, 0.0, x) - dot(jnp.where(inside, x, 0.0), w_all, ((1,), (0,)), HIGHEST)
        a_ref[rows(g), :] = w
        w_ref[rows(g), :] = jnp.zeros_like(w)

    w_ref[...] = jnp.zeros_like(w_ref)
    w = eliminate(a_ref[0:PIV, :], front(a_ref[0:PIV, :], 0), 0, lane)
    tile = update(a_ref[PIV : 2 * PIV, :], w, 0)

    def group(g, carry):
        w, tile = carry
        later = update(a_ref[rows(lax.rem(g + 1, groups)), :], w, g - 1)
        fresh = eliminate(tile, front(tile, g), g, lane)
        bulk(g - 1, w)
        return fresh, update(later, fresh, g)

    w, _ = lax.fori_loop(1, groups, group, (w, tile))
    bulk(groups - 1, w)


def helpers(axis, count):
    me = lax.axis_index(axis)

    def each(fn):
        def one(d, carry):
            fn(lax.rem(me + d, count))
            return carry
        lax.fori_loop(1, count, one, 0)

    def copy(p, src, buf, sems, slot):
        return pltpu.make_async_remote_copy(
            src_ref=src, dst_ref=buf.at[slot], send_sem=sems[0].at[p], recv_sem=sems[1].at[slot],
            device_id={axis: p}, device_id_type=MESH,
        )

    def send(src, buf, sems):
        each(lambda p: copy(p, src(p), buf, sems, me).start())

    def wait(buf, sems):
        each(lambda p: copy(p, buf.at[p], buf, sems, p).wait_recv())

    def drain(src, buf, sems):
        each(lambda p: copy(p, src(p), buf, sems, me).wait_send())

    def greet():
        each(lambda p: pl.semaphore_signal(
            pltpu.get_barrier_semaphore(), inc=1, device_id={axis: p}, device_id_type=MESH))

    return me, send, wait, drain, greet


def total_of(ref):
    return sum((ref[i] for i in range(1, ref.shape[0])), ref[0])


def first(nrow, ncol, frames, rf, cf, o_gram, o_cgram, o_total, o_rhs,
          slab, cgram, rpart, rrecv, rfull, rhs, *sems):
    slab_m, cg_m, rs_m, ag_m, rhs_m = (sems[2 * i : 2 * i + 2] for i in range(5))
    row, send_r, wait_r, drain_r, greet_r = helpers("row", nrow)
    col, send_c, wait_c, drain_c, greet_c = helpers("col", ncol)
    nb = frames.shape[0]
    rank = rf.shape[1]
    ch = rank // nrow
    greet_r()
    greet_c()
    gram = dot(rf[...], rf[...], ((0,), (0,)))
    for i in range(nrow):
        rpart[i] = gram[i * ch : (i + 1) * ch]
    rrecv[row] = rpart[row]
    cgram[col] = dot(cf[...], cf[...], ((0,), (0,)))
    pl.semaphore_wait(pltpu.get_barrier_semaphore(), nrow + ncol - 2)
    send_r(lambda p: rpart.at[p], rrecv, rs_m)
    send_c(lambda p: cgram.at[col], cgram, cg_m)

    def slab_one(b, carry):
        slab[col, b] = dot(frames[b], cf[...], ((1,), (0,)))
        return carry

    lax.fori_loop(0, nb, slab_one, 0)
    send_c(lambda p: slab.at[col], slab, slab_m)
    wait_r(rrecv, rs_m)
    rfull[row] = total_of(rrecv)
    send_r(lambda p: rfull.at[row], rfull, ag_m)
    wait_c(slab, slab_m)
    for b in range(nb):
        s = sum((slab[c, b] for c in range(1, ncol)), slab[0, b])
        o_total[b] = s
        rhs[row, b : b + 1, :] = jnp.sum(s * rf[...].astype(F32), axis=0, keepdims=True)
    rhs[row, nb:8, :] = jnp.zeros((8 - nb, rank), F32)
    send_r(lambda p: rhs.at[row], rhs, rhs_m)
    wait_c(cgram, cg_m)
    o_cgram[...] = total_of(cgram)
    wait_r(rfull, ag_m)
    for i in range(nrow):
        o_gram[i * ch : (i + 1) * ch, :] = rfull[i] * o_cgram[i * ch : (i + 1) * ch, :]
    wait_r(rhs, rhs_m)
    o_rhs[...] = total_of(rhs)
    drain_r(lambda p: rpart.at[p], rrecv, rs_m)
    drain_c(lambda p: cgram.at[col], cgram, cg_m)
    drain_c(lambda p: slab.at[col], slab, slab_m)
    drain_r(lambda p: rfull.at[row], rfull, ag_m)
    drain_r(lambda p: rhs.at[row], rhs, rhs_m)


def second(nb, gram, cgram, rhs, tgram, o_f, o_ff, o_time, o_mat, mat, w):
    mat[...] = gram[...]
    invert(mat, w)
    ff = dot(rhs[...], mat[...], ((1,), (0,)), HIGHEST)
    o_ff[...] = ff
    o_f[...] = ff[:nb]
    time_new = tgram[...] + dot(ff, ff, ((0,), (0,)), HIGHEST)
    o_time[...] = time_new
    o_mat[...] = time_new * cgram[...]


def third(nb, gram, ff, total, rhist, o_row, mat, w):
    mat[...] = gram[...]
    invert(mat, w)
    sums = rhist[...]
    for b in range(nb):
        sums = sums + ff[b : b + 1, :] * total[b]
    o_row[...] = dot(sums, mat[...], ((1,), (0,)), HIGHEST).astype(jnp.bfloat16)


def fourth(nrow, frames, new_row, ff, tnew, chist, o_mat, o_sum,
           gpart, grecv, gfull, ppart, precv, *sems):
    gs_m, ga_m, ps_m = (sems[2 * i : 2 * i + 2] for i in range(3))
    row, send, wait, drain, greet = helpers("row", nrow)
    nb, _, cols = frames.shape
    rank = ff.shape[1]
    ch, pch = rank // nrow, cols // nrow
    greet()
    gram = dot(new_row[...], new_row[...], ((0,), (0,)))
    for i in range(nrow):
        gpart[i] = gram[i * ch : (i + 1) * ch]
    grecv[row] = gpart[row]
    pl.semaphore_wait(pltpu.get_barrier_semaphore(), nrow - 1)
    send(lambda p: gpart.at[p], grecv, gs_m)
    wide = 256
    for j in range(0, cols, wide):
        acc = jnp.zeros((wide, rank), F32)
        for b in range(nb):
            acc = acc + ff[b : b + 1, :] * dot(
                frames[b, :, j : j + wide], new_row[...], ((0,), (0,))
            )
        acc = acc.astype(jnp.bfloat16)
        for i in range(wide // pch):
            ppart[j // pch + i] = acc[i * pch : (i + 1) * pch]
    wait(grecv, gs_m)
    gfull[row] = total_of(grecv)
    send(lambda p: gfull.at[row], gfull, ga_m)
    precv[row] = ppart[row]
    send(lambda p: ppart.at[p], precv, ps_m)
    wait(gfull, ga_m)
    for i in range(nrow):
        o_mat[i * ch : (i + 1) * ch, :] = gfull[i] * tnew[i * ch : (i + 1) * ch, :]
    wait(precv, ps_m)
    own = chist[pl.ds(pl.multiple_of(row * pch, pch), pch), :]
    for i in range(nrow):
        own = own + precv[i].astype(F32)
    o_sum[...] = own
    drain(lambda p: gpart.at[p], grecv, gs_m)
    drain(lambda p: gfull.at[row], gfull, ga_m)
    drain(lambda p: ppart.at[p], precv, ps_m)


def fifth(gram, own, o_own, mat, w):
    mat[...] = gram[...]
    invert(mat, w)
    o_own[...] = dot(own[...], mat[...], ((1,), (0,)), HIGHEST).astype(jnp.bfloat16)


def sixth(nrow, own, o_col, pfull, *pa_m):
    row, send, wait, drain, greet = helpers("row", nrow)
    pch = own.shape[0]
    greet()
    pfull[row] = own[...]
    pl.semaphore_wait(pltpu.get_barrier_semaphore(), nrow - 1)
    send(lambda p: pfull.at[row], pfull, pa_m)
    wait(pfull, pa_m)
    for i in range(nrow):
        o_col[i * pch : (i + 1) * pch, :] = pfull[i]
    drain(lambda p: pfull.at[row], pfull, pa_m)


def body(nrow, ncol, frames, rf, cf, rhist, chist, tgram):
    nb, rows, cols = frames.shape
    rank = rf.shape[1]
    ch, pch = rank // nrow, cols // nrow
    vm = pltpu.VMEM
    bf = jnp.bfloat16
    space = pl.BlockSpec(memory_space=vm)
    shape = jax.ShapeDtypeStruct
    square = shape((rank, rank), F32)

    def sems(*counts):
        return [pltpu.SemaphoreType.DMA((c,)) for c in counts for _ in range(2)]

    def call(fn, name, outs, scratch, args, collective=None):
        remote = {} if collective is None else dict(collective_id=collective, has_side_effects=True)
        return pl.pallas_call(
            fn, out_shape=outs, in_specs=[space] * len(args), out_specs=(space,) * len(outs),
            scratch_shapes=scratch, name=name,
            compiler_params=pltpu.CompilerParams(vmem_limit_bytes=48 * 1024 * 1024, **remote),
        )(*args)

    block = vm((nrow, ch, rank), F32)
    gram, cgram, total, rhs = call(
        functools.partial(first, nrow, ncol), "first",
        (square, square, shape((nb, rows, rank), F32), shape((8, rank), F32)),
        [vm((ncol, nb, rows, rank), F32), vm((ncol, rank, rank), F32), block, block, block,
         vm((nrow, 8, rank), F32)] + sems(ncol, ncol, nrow, nrow, nrow),
        (frames, rf, cf), 0)
    local = [vm((rank, rank), F32)] * 2
    f, ff, tnew, mat = call(
        functools.partial(second, nb), "second",
        (shape((nb, rank), F32), shape((8, rank), F32), square, square), local, (gram, cgram, rhs, tgram))
    new_row, = call(
        functools.partial(third, nb), "third", (shape((rows, rank), bf),), local, (mat, ff, total, rhist))
    part = vm((nrow, pch, rank), bf)
    mat, own = call(
        functools.partial(fourth, nrow), "fourth", (square, shape((pch, rank), F32)),
        [block, block, block, part, part] + sems(nrow, nrow, nrow),
        (frames, new_row, ff, tnew, chist), 1)
    own, = call(fifth, "fifth", (shape((pch, rank), bf),), local, (mat, own))
    new_col, = call(
        functools.partial(sixth, nrow), "sixth", (shape((cols, rank), bf),), [part] + sems(nrow), (own,), 2)
    return f, new_row, new_col


def solution(mesh):
    in_specs = (
        P(None, "row", "col"),
        P("row", None),
        P("col", None),
        P("row", None),
        P("col", None),
        P(),
    )
    out_specs = (P(), P("row", None), P("col", None))
    return jax.shard_map(
        functools.partial(body, mesh.shape["row"], mesh.shape["col"]),
        mesh=mesh, in_specs=in_specs, out_specs=out_specs, check_vma=False,
    )
```

```python
import functools

import jax
import jax.numpy as jnp
from jax import lax
from jax.experimental import pallas as pl
from jax.experimental.pallas import tpu as pltpu
from jax.sharding import PartitionSpec as P

MESH = pl.DeviceIdType.MESH
HIGHEST = lax.Precision.HIGHEST
F32 = jnp.float32
PIV = 8


def dot(a, b, dims, precision=None):
    return lax.dot_general(a, b, (dims, ((), ())), precision=precision, preferred_element_type=F32)


def eliminate(tile, turned, g, lane):
    n = tile.shape[1]
    wide = (PIV, 128)
    sub = lax.broadcasted_iota(jnp.int32, wide, 0)
    cols = [jnp.broadcast_to(turned[:, b : b + 1], wide) for b in range(PIV)]
    for k in range(PIV):
        row = [jnp.broadcast_to(c[k : k + 1, :], wide) for c in cols]
        p = 1.0 / row[k]
        ck = cols[k]
        here = sub == k
        for b in range(PIV):
            if b == k:
                cols[b] = jnp.where(here, p, -(ck * p))
            else:
                w = row[b] * p
                cols[b] = jnp.where(here, w, cols[b] - ck * w)
    at = lane - g * PIV
    unit = (at == lax.broadcasted_iota(jnp.int32, (PIV, n), 0)).astype(F32)
    tile = jnp.where((at >= 0) & (at < PIV), unit, tile)
    out = None
    for b in range(PIV):
        scale = jnp.concatenate([cols[b]] * (n // 128), axis=1)
        term = scale * jnp.broadcast_to(tile[b : b + 1, :], (PIV, n))
        out = term if out is None else out + term
    return out


def invert(a_ref, w_ref):
    n = a_ref.shape[0]
    groups = n // PIV
    lane = lax.broadcasted_iota(jnp.int32, (PIV, n), 1)
    lanes = lax.broadcasted_iota(jnp.int32, (n, n), 1)

    def rows(g):
        return pl.ds(pl.multiple_of(g * PIV, PIV), PIV)

    def front(tile, g):
        return pltpu.roll(tile, lax.rem(n - g * PIV, n), 1)

    def update(tile, w, g):
        turned = front(tile, g)
        y = jnp.where((lane >= g * PIV) & (lane < g * PIV + PIV), 0.0, tile)
        for a in range(PIV):
            y = y - jnp.broadcast_to(turned[:, a : a + 1], y.shape) * jnp.broadcast_to(w[a : a + 1, :], y.shape)
        return y

    def bulk(g, w):
        w_ref[rows(g), :] = w
        inside = (lanes >= g * PIV) & (lanes < g * PIV + PIV)
        x = a_ref[...]
        w_all = w_ref[...]
        a_ref[...] = jnp.where(inside, 0.0, x) - dot(jnp.where(inside, x, 0.0), w_all, ((1,), (0,)), HIGHEST)
        a_ref[rows(g), :] = w
        w_ref[rows(g), :] = jnp.zeros_like(w)

    w_ref[...] = jnp.zeros_like(w_ref)
    w = eliminate(a_ref[0:PIV, :], front(a_ref[0:PIV, :], 0), 0, lane)
    tile = update(a_ref[PIV : 2 * PIV, :], w, 0)

    def group(g, carry):
        w, tile = carry
        later = update(a_ref[rows(lax.rem(g + 1, groups)), :], w, g - 1)
        fresh = eliminate(tile, front(tile, g), g, lane)
        bulk(g - 1, w)
        return fresh, update(later, fresh, g)

    w, _ = lax.fori_loop(1, groups, group, (w, tile))
    bulk(groups - 1, w)


def helpers(axis, count):
    me = lax.axis_index(axis)

    def each(fn):
        def one(d, carry):
            fn(lax.rem(me + d, count))
            return carry
        lax.fori_loop(1, count, one, 0)

    def copy(p, src, buf, sems, slot):
        return pltpu.make_async_remote_copy(
            src_ref=src, dst_ref=buf.at[slot], send_sem=sems[0].at[p], recv_sem=sems[1].at[slot],
            device_id={axis: p}, device_id_type=MESH,
        )

    def send(src, buf, sems):
        each(lambda p: copy(p, src(p), buf, sems, me).start())

    def wait(buf, sems):
        each(lambda p: copy(p, buf.at[p], buf, sems, p).wait_recv())

    def drain(src, buf, sems):
        each(lambda p: copy(p, src(p), buf, sems, me).wait_send())

    def greet():
        each(lambda p: pl.semaphore_signal(
            pltpu.get_barrier_semaphore(), inc=1, device_id={axis: p}, device_id_type=MESH))

    return me, send, wait, drain, greet


def total_of(ref):
    return sum((ref[i] for i in range(1, ref.shape[0])), ref[0])


def kernel(nrow, ncol, share, frames, rf, cf, rhist, chist, tgram, o_f, o_row, o_col,
           slab, cgram, gall, recv, full, hall, hrecv, hfull, rhs, ppart, precv, pfull,
           total, mat, w, tnew, *sems):
    (slab_m, cg_m, rs_m, ag_m, ax_m, rhs_m, gs_m, ga_m, gx_m, ps_m, pa_m) = (
        sems[2 * i : 2 * i + 2] for i in range(11)
    )
    row, send_r, wait_r, drain_r, greet_r = helpers("row", nrow)
    col, send_c, wait_c, drain_c, greet_c = helpers("col", ncol)
    nb, _, cols = frames.shape
    rank = rf.shape[1]
    ch, pch = rank // nrow // share, cols // nrow
    mine = col if share > 1 else 0

    def gram_start(x, everything, got):
        gram = dot(x, x, ((0,), (0,)))
        for i in range(nrow * share):
            everything[i] = gram[i * ch : (i + 1) * ch]
        got[row] = everything[mine * nrow + row]

    def gram_scatter(everything, got, m):
        send_r(lambda p: everything.at[mine * nrow + p], got, m)

    def gram_gather(got, whole, m_in, m_out):
        wait_r(got, m_in)
        whole[mine, row] = total_of(got)
        send_r(lambda p: whole.at[mine, row], whole.at[mine], m_out)

    def gram_times(whole, other, m_in, m_x):
        wait_r(whole.at[mine], m_in)
        if share > 1:
            send_c(lambda p: whole.at[col], whole, m_x)
            wait_c(whole, m_x)
        for c in range(share):
            for i in range(nrow):
                at = (c * nrow + i) * ch
                mat[at : at + ch, :] = whole[c, i] * other[at : at + ch, :]

    def gram_drain(everything, got, whole, m_s, m_a, m_x):
        drain_r(lambda p: everything.at[mine * nrow + p], got, m_s)
        drain_r(lambda p: whole.at[mine, row], whole.at[mine], m_a)
        if share > 1:
            drain_c(lambda p: whole.at[col], whole, m_x)

    greet_r()
    greet_c()
    gram_start(rf[...], gall, recv)
    cgram[col] = dot(cf[...], cf[...], ((0,), (0,)))
    pl.semaphore_wait(pltpu.get_barrier_semaphore(), nrow + ncol - 2)
    gram_scatter(gall, recv, rs_m)
    send_c(lambda p: cgram.at[col], cgram, cg_m)

    def slab_one(b, carry):
        slab[col, b] = dot(frames[b], cf[...], ((1,), (0,)))
        return carry

    lax.fori_loop(0, nb, slab_one, 0)
    gram_gather(recv, full, rs_m, ag_m)
    send_c(lambda p: slab.at[col], slab, slab_m)
    wait_c(cgram, cg_m)
    tnew[...] = total_of(cgram)
    wait_c(slab, slab_m)
    for b in range(nb):
        s = sum((slab[c, b] for c in range(1, ncol)), slab[0, b])
        total[b] = s
        rhs[row, b : b + 1, :] = jnp.sum(s * rf[...].astype(F32), axis=0, keepdims=True)
    rhs[row, nb:8, :] = jnp.zeros((8 - nb, rank), F32)
    gram_times(full, tnew, ag_m, ax_m)
    send_r(lambda p: rhs.at[row], rhs, rhs_m)
    invert(mat, w)
    wait_r(rhs, rhs_m)
    ff = dot(total_of(rhs), mat[...], ((1,), (0,)), HIGHEST)
    o_f[...] = ff[:nb]

    time_new = tgram[...] + dot(ff, ff, ((0,), (0,)), HIGHEST)
    mat[...] = time_new * tnew[...]
    tnew[...] = time_new
    invert(mat, w)
    sums = rhist[...]
    for b in range(nb):
        sums = sums + ff[b : b + 1, :] * total[b]
    new_row = dot(sums, mat[...], ((1,), (0,)), HIGHEST).astype(jnp.bfloat16)
    o_row[...] = new_row

    gram_start(new_row, hall, hrecv)
    gram_scatter(hall, hrecv, gs_m)
    wide = 256

    def products(j):
        acc = jnp.zeros((wide, rank), F32)
        for b in range(nb):
            acc = acc + ff[b : b + 1, :] * dot(frames[b, :, j : j + wide], new_row, ((0,), (0,)))
        acc = acc.astype(jnp.bfloat16)
        for i in range(wide // pch):
            ppart[j // pch + i] = acc[i * pch : (i + 1) * pch]

    half = cols // 2
    for j in range(0, half, wide):
        products(j)
    gram_gather(hrecv, hfull, gs_m, ga_m)
    for j in range(half, cols, wide):
        products(j)
    gram_times(hfull, tnew, ga_m, gx_m)
    precv[row] = ppart[row]
    send_r(lambda p: ppart.at[p], precv, ps_m)
    invert(mat, w)
    wait_r(precv, ps_m)
    own = chist[pl.ds(pl.multiple_of(row * pch, pch), pch), :]
    for i in range(nrow):
        own = own + precv[i].astype(F32)
    pfull[row] = dot(own, mat[...], ((1,), (0,)), HIGHEST).astype(jnp.bfloat16)
    send_r(lambda p: pfull.at[row], pfull, pa_m)

    drain_c(lambda p: cgram.at[col], cgram, cg_m)
    drain_c(lambda p: slab.at[col], slab, slab_m)
    gram_drain(gall, recv, full, rs_m, ag_m, ax_m)
    drain_r(lambda p: rhs.at[row], rhs, rhs_m)
    gram_drain(hall, hrecv, hfull, gs_m, ga_m, gx_m)
    drain_r(lambda p: ppart.at[p], precv, ps_m)
    wait_r(pfull, pa_m)
    for i in range(nrow):
        o_col[i * pch : (i + 1) * pch, :] = pfull[i]
    drain_r(lambda p: pfull.at[row], pfull, pa_m)


def body(nrow, ncol, frames, rf, cf, rhist, chist, tgram):
    nb, rows, cols = frames.shape
    rank = rf.shape[1]
    share = ncol if rank % (8 * nrow * ncol) == 0 else 1
    ch, pch = rank // nrow // share, cols // nrow
    vm = pltpu.VMEM
    bf = jnp.bfloat16
    space = pl.BlockSpec(memory_space=vm)
    shape = jax.ShapeDtypeStruct
    counts = [ncol, ncol, nrow, nrow, ncol, nrow, nrow, nrow, ncol, nrow, nrow]
    square = vm((rank, rank), F32)
    part = vm((nrow, pch, rank), bf)
    gram = [
        vm((nrow * share, ch, rank), F32),
        vm((nrow, ch, rank), F32),
        vm((share, nrow, ch, rank), F32),
    ]
    return pl.pallas_call(
        functools.partial(kernel, nrow, ncol, share),
        out_shape=(shape((nb, rank), F32), shape((rows, rank), bf), shape((cols, rank), bf)),
        in_specs=[space] * 6,
        out_specs=(space,) * 3,
        scratch_shapes=[
            vm((ncol, nb, rows, rank), F32), vm((ncol, rank, rank), F32), *gram, *gram,
            vm((nrow, 8, rank), F32), part, part, part,
            vm((nb, rows, rank), F32), square, square, square,
        ] + [pltpu.SemaphoreType.DMA((c,)) for c in counts for _ in range(2)],
        compiler_params=pltpu.CompilerParams(
            collective_id=0, has_side_effects=True, vmem_limit_bytes=48 * 1024 * 1024
        ),
    )(frames, rf, cf, rhist, chist, tgram)


def solution(mesh):
    in_specs = (
        P(None, "row", "col"),
        P("row", None),
        P("col", None),
        P("row", None),
        P("col", None),
        P(),
    )
    out_specs = (P(), P("row", None), P("col", None))
    return jax.shard_map(
        functools.partial(body, mesh.shape["row"], mesh.shape["col"]),
        mesh=mesh, in_specs=in_specs, out_specs=out_specs, check_vma=False,
    )
```

```python
import functools

import jax
import jax.numpy as jnp
from jax import lax
from jax.experimental import pallas as pl
from jax.experimental.pallas import tpu as pltpu
from jax.sharding import PartitionSpec as P

MESH = pl.DeviceIdType.MESH
HIGHEST = lax.Precision.HIGHEST
F32 = jnp.float32
PIV = 8


def dot(a, b, dims, precision=None):
    return lax.dot_general(a, b, (dims, ((), ())), precision=precision, preferred_element_type=F32)


def eliminate(cols):
    cols = list(cols)
    sub = lax.broadcasted_iota(jnp.int32, cols[0].shape, 0)
    for k in range(PIV):
        row = [jnp.broadcast_to(c[k : k + 1, :], c.shape) for c in cols]
        p = 1.0 / row[k]
        ck = cols[k]
        here = sub == k
        for b in range(len(cols)):
            if b == k:
                cols[b] = jnp.where(here, p, -(ck * p))
            else:
                w = row[b] * p
                cols[b] = jnp.where(here, w, cols[b] - ck * w)
    return cols


def add_up(terms):
    while len(terms) > 1:
        terms = [sum(terms[i : i + 2][1:], terms[i]) for i in range(0, len(terms), 2)]
    return terms[0]


def invert(a_ref, w_ref):
    n = a_ref.shape[0]
    groups = n // PIV
    lane = lax.broadcasted_iota(jnp.int32, (PIV, n), 1)
    lanes = lax.broadcasted_iota(jnp.int32, (n, n), 1)

    def rows(g):
        return pl.ds(pl.multiple_of(g * PIV, PIV), PIV)

    def columns(tile, g):
        turned = pltpu.roll(tile, lax.rem(2 * n - g * PIV, n), 1)
        return [jnp.broadcast_to(turned[:, b : b + 1], (PIV, 128)) for b in range(PIV)]

    def wide(c):
        return jnp.concatenate([c] * (n // 128), axis=1) if n > 128 else c

    def times(cols, tile):
        return add_up([wide(cols[b]) * jnp.broadcast_to(tile[b : b + 1, :], (PIV, n)) for b in range(PIV)])

    def within(g, iota):
        return (iota >= g * PIV) & (iota < g * PIV + PIV)

    def update(tile, cols, w, g):
        return jnp.where(within(g, lane), 0.0, tile) - times(cols, w)

    def advance(g, tile, block, later):
        ahead = columns(later, g + 1)
        mult = columns(later, g)
        cols = eliminate(list(block) + columns(tile, g + 1))
        unit = (lane - g * PIV == lax.broadcasted_iota(jnp.int32, (PIV, n), 0)).astype(F32)
        w = times(cols[:PIV], jnp.where(within(g, lane), unit, tile))
        new_block = tuple(
            ahead[b] - add_up([mult[a] * jnp.broadcast_to(cols[PIV + b][a : a + 1, :], (PIV, 128)) for a in range(PIV)])
            for b in range(PIV)
        )
        return w, update(later, mult, w, g), new_block

    def bulk(g, w):
        w_ref[rows(g), :] = w
        inside = within(g, lanes)
        x = a_ref[...]
        a_ref[...] = jnp.where(inside, 0.0, x) - dot(
            jnp.where(inside, x, 0.0), w_ref[...], ((1,), (0,)), HIGHEST
        )
        a_ref[rows(g), :] = w
        w_ref[rows(g), :] = jnp.zeros_like(w)

    w_ref[...] = jnp.zeros_like(w_ref)
    tile = a_ref[0:PIV, :]
    carry = advance(0, tile, columns(tile, 0), a_ref[PIV : 2 * PIV, :])

    def group(g, carry):
        w, tile, block = carry
        later = a_ref[rows(lax.rem(g + 1, groups)), :]
        later = update(later, columns(later, g - 1), w, g - 1)
        out = advance(g, tile, block, later)
        bulk(g - 1, w)
        return out

    w = lax.fori_loop(1, groups, group, carry)[0]
    bulk(groups - 1, w)


def factor(mat, below, w):
    h = mat.shape[0] // 2
    top = mat.at[0:h, 0:h]
    rest = mat.at[h : 2 * h, h : 2 * h]
    invert(top, w)
    below[...] = dot(mat[h : 2 * h, 0:h], top[...], ((1,), (0,)), HIGHEST)
    rest[...] = rest[...] - dot(below[...], mat[0:h, h : 2 * h], ((1,), (0,)), HIGHEST)
    invert(rest, w)


def solve(rhs, mat, below):
    h = mat.shape[0] // 2
    one, two = rhs[:, 0:h], rhs[:, h : 2 * h]
    two = two - dot(one, below[...], ((1,), (1,)), HIGHEST)
    two = dot(two, mat[h : 2 * h, h : 2 * h], ((1,), (0,)), HIGHEST)
    one = dot(one, mat[0:h, 0:h], ((1,), (0,)), HIGHEST) - dot(two, below[...], ((1,), (0,)), HIGHEST)
    return jnp.concatenate([one, two], axis=1)


def helpers(axis, count):
    me = lax.axis_index(axis)

    def each(fn):
        def one(d, carry):
            fn(lax.rem(me + d, count))
            return carry
        lax.fori_loop(1, count, one, 0)

    def copy(p, src, buf, sems, slot):
        return pltpu.make_async_remote_copy(
            src_ref=src, dst_ref=buf.at[slot], send_sem=sems[0].at[p], recv_sem=sems[1].at[slot],
            device_id={axis: p}, device_id_type=MESH,
        )

    def send(src, buf, sems):
        each(lambda p: copy(p, src(p), buf, sems, me).start())

    def wait(buf, sems):
        each(lambda p: copy(p, buf.at[p], buf, sems, p).wait_recv())

    def drain(src, buf, sems):
        each(lambda p: copy(p, src(p), buf, sems, me).wait_send())

    def greet():
        each(lambda p: pl.semaphore_signal(
            pltpu.get_barrier_semaphore(), inc=1, device_id={axis: p}, device_id_type=MESH))

    return me, send, wait, drain, greet


def total_of(ref):
    return sum((ref[i] for i in range(1, ref.shape[0])), ref[0])


def kernel(nrow, ncol, share, frames, rf, cf, rhist, chist, tgram, o_f, o_row, o_col,
           slab, cgram, gall, recv, full, hall, hrecv, hfull, rhs, ppart, precv, pfull,
           total, mat, w, below, tnew, *sems):
    (slab_m, cg_m, rs_m, ag_m, ax_m, rhs_m, gs_m, ga_m, gx_m, ps_m, pa_m) = (
        sems[2 * i : 2 * i + 2] for i in range(11)
    )
    row, send_r, wait_r, drain_r, greet_r = helpers("row", nrow)
    col, send_c, wait_c, drain_c, greet_c = helpers("col", ncol)
    nb, _, cols = frames.shape
    rank = rf.shape[1]
    ch, pch = rank // nrow // share, cols // nrow
    mine = col if share > 1 else 0

    def gram_start(x, everything, got):
        gram = dot(x, x, ((0,), (0,)))
        for i in range(nrow * share):
            everything[i] = gram[i * ch : (i + 1) * ch]
        got[row] = everything[mine * nrow + row]

    def gram_scatter(everything, got, m):
        send_r(lambda p: everything.at[mine * nrow + p], got, m)

    def gram_gather(got, whole, m_in, m_out):
        wait_r(got, m_in)
        whole[mine, row] = total_of(got)
        send_r(lambda p: whole.at[mine, row], whole.at[mine], m_out)

    def gram_times(whole, other, m_in, m_x):
        wait_r(whole.at[mine], m_in)
        if share > 1:
            send_c(lambda p: whole.at[col], whole, m_x)
            wait_c(whole, m_x)
        for c in range(share):
            for i in range(nrow):
                at = (c * nrow + i) * ch
                mat[at : at + ch, :] = whole[c, i] * other[at : at + ch, :]

    def gram_drain(everything, got, whole, m_s, m_a, m_x):
        drain_r(lambda p: everything.at[mine * nrow + p], got, m_s)
        drain_r(lambda p: whole.at[mine, row], whole.at[mine], m_a)
        if share > 1:
            drain_c(lambda p: whole.at[col], whole, m_x)

    greet_r()
    greet_c()
    gram_start(rf[...], gall, recv)
    cgram[col] = dot(cf[...], cf[...], ((0,), (0,)))
    pl.semaphore_wait(pltpu.get_barrier_semaphore(), nrow + ncol - 2)
    gram_scatter(gall, recv, rs_m)
    send_c(lambda p: cgram.at[col], cgram, cg_m)

    def slab_one(b, carry):
        slab[col, b] = dot(frames[b], cf[...], ((1,), (0,)))
        return carry

    lax.fori_loop(0, nb, slab_one, 0)
    gram_gather(recv, full, rs_m, ag_m)
    send_c(lambda p: slab.at[col], slab, slab_m)
    wait_c(cgram, cg_m)
    tnew[...] = total_of(cgram)
    wait_c(slab, slab_m)
    for b in range(nb):
        s = sum((slab[c, b] for c in range(1, ncol)), slab[0, b])
        total[b] = s
        rhs[row, b : b + 1, :] = jnp.sum(s * rf[...].astype(F32), axis=0, keepdims=True)
    rhs[row, nb:8, :] = jnp.zeros((8 - nb, rank), F32)
    gram_times(full, tnew, ag_m, ax_m)
    send_r(lambda p: rhs.at[row], rhs, rhs_m)
    factor(mat, below, w)
    wait_r(rhs, rhs_m)
    ff = solve(total_of(rhs), mat, below)
    o_f[...] = ff[:nb]

    time_new = tgram[...] + dot(ff, ff, ((0,), (0,)), HIGHEST)
    mat[...] = time_new * tnew[...]
    tnew[...] = time_new
    factor(mat, below, w)
    sums = rhist[...]
    for b in range(nb):
        sums = sums + ff[b : b + 1, :] * total[b]
    new_row = solve(sums, mat, below).astype(jnp.bfloat16)
    o_row[...] = new_row

    gram_start(new_row, hall, hrecv)
    gram_scatter(hall, hrecv, gs_m)
    wide = 256

    def products(j):
        acc = jnp.zeros((wide, rank), F32)
        for b in range(nb):
            acc = acc + ff[b : b + 1, :] * dot(frames[b, :, j : j + wide], new_row, ((0,), (0,)))
        acc = acc.astype(jnp.bfloat16)
        for i in range(wide // pch):
            ppart[j // pch + i] = acc[i * pch : (i + 1) * pch]

    half = cols // 2
    for j in range(0, half, wide):
        products(j)
    gram_gather(hrecv, hfull, gs_m, ga_m)
    for j in range(half, cols, wide):
        products(j)
    gram_times(hfull, tnew, ga_m, gx_m)
    precv[row] = ppart[row]
    send_r(lambda p: ppart.at[p], precv, ps_m)
    factor(mat, below, w)
    wait_r(precv, ps_m)
    own = chist[pl.ds(pl.multiple_of(row * pch, pch), pch), :]
    for i in range(nrow):
        own = own + precv[i].astype(F32)
    pfull[row] = solve(own, mat, below).astype(jnp.bfloat16)
    send_r(lambda p: pfull.at[row], pfull, pa_m)

    drain_c(lambda p: cgram.at[col], cgram, cg_m)
    drain_c(lambda p: slab.at[col], slab, slab_m)
    gram_drain(gall, recv, full, rs_m, ag_m, ax_m)
    drain_r(lambda p: rhs.at[row], rhs, rhs_m)
    gram_drain(hall, hrecv, hfull, gs_m, ga_m, gx_m)
    drain_r(lambda p: ppart.at[p], precv, ps_m)
    wait_r(pfull, pa_m)
    for i in range(nrow):
        o_col[i * pch : (i + 1) * pch, :] = pfull[i]
    drain_r(lambda p: pfull.at[row], pfull, pa_m)


def body(nrow, ncol, frames, rf, cf, rhist, chist, tgram):
    nb, rows, cols = frames.shape
    rank = rf.shape[1]
    share = ncol if rank % (8 * nrow * ncol) == 0 else 1
    ch, pch = rank // nrow // share, cols // nrow
    vm = pltpu.VMEM
    bf = jnp.bfloat16
    space = pl.BlockSpec(memory_space=vm)
    shape = jax.ShapeDtypeStruct
    counts = [ncol, ncol, nrow, nrow, ncol, nrow, nrow, nrow, ncol, nrow, nrow]
    square = vm((rank, rank), F32)
    quarter = vm((rank // 2, rank // 2), F32)
    part = vm((nrow, pch, rank), bf)
    gram = [
        vm((nrow * share, ch, rank), F32),
        vm((nrow, ch, rank), F32),
        vm((share, nrow, ch, rank), F32),
    ]
    return pl.pallas_call(
        functools.partial(kernel, nrow, ncol, share),
        out_shape=(shape((nb, rank), F32), shape((rows, rank), bf), shape((cols, rank), bf)),
        in_specs=[space] * 6,
        out_specs=(space,) * 3,
        scratch_shapes=[
            vm((ncol, nb, rows, rank), F32), vm((ncol, rank, rank), F32), *gram, *gram,
            vm((nrow, 8, rank), F32), part, part, part,
            vm((nb, rows, rank), F32), square, quarter, quarter, square,
        ] + [pltpu.SemaphoreType.DMA((c,)) for c in counts for _ in range(2)],
        compiler_params=pltpu.CompilerParams(
            collective_id=0, has_side_effects=True, vmem_limit_bytes=48 * 1024 * 1024
        ),
    )(frames, rf, cf, rhist, chist, tgram)


def solution(mesh):
    in_specs = (
        P(None, "row", "col"),
        P("row", None),
        P("col", None),
        P("row", None),
        P("col", None),
        P(),
    )
    out_specs = (P(), P("row", None), P("col", None))
    return jax.shard_map(
        functools.partial(body, mesh.shape["row"], mesh.shape["col"]),
        mesh=mesh, in_specs=in_specs, out_specs=out_specs, check_vma=False,
    )
```

```python
import functools

import jax
import jax.numpy as jnp
from jax import lax
from jax.experimental import pallas as pl
from jax.experimental.pallas import tpu as pltpu
from jax.sharding import PartitionSpec as P

MESH = pl.DeviceIdType.MESH
HIGHEST = lax.Precision.HIGHEST
F32 = jnp.float32
VMEM_BYTES = 62 * 1024 * 1024
PIV = 8


def dot(a, b, dims, precision=None):
    return lax.dot_general(a, b, (dims, ((), ())), precision=precision, preferred_element_type=F32)


def reciprocal(x):
    r = pl.reciprocal(x, approx=True)
    for _ in range(2):
        r = r + r * (1.0 - x * r)
    return r


def eliminate(cols):
    cols = list(cols)
    sub = lax.broadcasted_iota(jnp.int32, cols[0].shape, 0)
    for k in range(PIV):
        row = [jnp.broadcast_to(c[k : k + 1, :], c.shape) for c in cols]
        p = reciprocal(row[k])
        ck = cols[k]
        here = sub == k
        for b in range(len(cols)):
            if b == k:
                cols[b] = jnp.where(here, p, -(ck * p))
            else:
                w = row[b] * p
                cols[b] = jnp.where(here, w, cols[b] - ck * w)
    return cols


def add_up(terms):
    while len(terms) > 1:
        terms = [sum(terms[i : i + 2][1:], terms[i]) for i in range(0, len(terms), 2)]
    return terms[0]


def invert(a_ref, w_ref):
    n = a_ref.shape[0]
    groups = n // PIV
    lane = lax.broadcasted_iota(jnp.int32, (PIV, n), 1)
    lanes = lax.broadcasted_iota(jnp.int32, (n, n), 1)

    def rows(g):
        return pl.ds(pl.multiple_of(g * PIV, PIV), PIV)

    def columns(tile, g):
        turned = pltpu.roll(tile, lax.rem(2 * n - g * PIV, n), 1)
        return [jnp.broadcast_to(turned[:, b : b + 1], (PIV, 128)) for b in range(PIV)]

    def wide(c):
        return jnp.concatenate([c] * (n // 128), axis=1) if n > 128 else c

    def times(cols, tile):
        return add_up([wide(cols[b]) * jnp.broadcast_to(tile[b : b + 1, :], (PIV, n)) for b in range(PIV)])

    def within(g, iota):
        return (iota >= g * PIV) & (iota < g * PIV + PIV)

    def update(tile, cols, w, g):
        return jnp.where(within(g, lane), 0.0, tile) - times(cols, w)

    def advance(g, tile, block, later):
        ahead = columns(later, g + 1)
        mult = columns(later, g)
        cols = eliminate(list(block) + columns(tile, g + 1))
        unit = (lane - g * PIV == lax.broadcasted_iota(jnp.int32, (PIV, n), 0)).astype(F32)
        w = times(cols[:PIV], jnp.where(within(g, lane), unit, tile))
        new_block = tuple(
            ahead[b] - add_up([mult[a] * jnp.broadcast_to(cols[PIV + b][a : a + 1, :], (PIV, 128)) for a in range(PIV)])
            for b in range(PIV)
        )
        return w, update(later, mult, w, g), new_block

    def bulk(g, w):
        w_ref[rows(g), :] = w
        inside = within(g, lanes)
        x = a_ref[...]
        a_ref[...] = jnp.where(inside, 0.0, x) - dot(
            jnp.where(inside, x, 0.0), w_ref[...], ((1,), (0,)), HIGHEST
        )
        a_ref[rows(g), :] = w
        w_ref[rows(g), :] = jnp.zeros_like(w)

    w_ref[...] = jnp.zeros_like(w_ref)
    tile = a_ref[0:PIV, :]
    carry = advance(0, tile, columns(tile, 0), a_ref[PIV : 2 * PIV, :])

    def group(g, carry):
        w, tile, block = carry
        later = a_ref[rows(lax.rem(g + 1, groups)), :]
        later = update(later, columns(later, g - 1), w, g - 1)
        out = advance(g, tile, block, later)
        bulk(g - 1, w)
        return out

    w = lax.fori_loop(1, groups, group, carry)[0]
    bulk(groups - 1, w)


def factor(mat, below, w):
    h = mat.shape[0] // 2
    top = mat.at[0:h, 0:h]
    rest = mat.at[h : 2 * h, h : 2 * h]
    invert(top, w)
    below[...] = dot(mat[h : 2 * h, 0:h], top[...], ((1,), (0,)), HIGHEST)
    rest[...] = rest[...] - dot(below[...], mat[0:h, h : 2 * h], ((1,), (0,)), HIGHEST)
    invert(rest, w)


def solve(rhs, mat, below):
    h = mat.shape[0] // 2
    one, two = rhs[:, 0:h], rhs[:, h : 2 * h]
    two = two - dot(one, below[...], ((1,), (1,)), HIGHEST)
    two = dot(two, mat[h : 2 * h, h : 2 * h], ((1,), (0,)), HIGHEST)
    one = dot(one, mat[0:h, 0:h], ((1,), (0,)), HIGHEST) - dot(two, below[...], ((1,), (0,)), HIGHEST)
    return jnp.concatenate([one, two], axis=1)


def helpers(axis, count):
    me = lax.axis_index(axis)

    def each(fn):
        def one(d, carry):
            fn(lax.rem(me + d, count))
            return carry
        lax.fori_loop(1, count, one, 0)

    def copy(p, src, buf, sems, slot):
        return pltpu.make_async_remote_copy(
            src_ref=src, dst_ref=buf.at[slot], send_sem=sems[0].at[p], recv_sem=sems[1].at[slot],
            device_id={axis: p}, device_id_type=MESH,
        )

    def send(src, buf, sems):
        each(lambda p: copy(p, src(p), buf, sems, me).start())

    def wait(buf, sems):
        each(lambda p: copy(p, buf.at[p], buf, sems, p).wait_recv())

    def drain(src, buf, sems):
        each(lambda p: copy(p, src(p), buf, sems, me).wait_send())

    def greet():
        each(lambda p: pl.semaphore_signal(
            pltpu.get_barrier_semaphore(), inc=1, device_id={axis: p}, device_id_type=MESH))

    return me, send, wait, drain, greet


def total_of(ref):
    return sum((ref[i] for i in range(1, ref.shape[0])), ref[0])


def kernel(nrow, ncol, share, frames_h, rf_h, cf_h, rhist_h, chist_h, tgram_h,
           o_f, o_row, o_col, frames, rf, cf, rhist, chist, tgram, in_s, slab, cgram, gall, recv, full, hall, hrecv, hfull, rhs, ppart, precv, pfull,
           total, mat, w, below, tnew, *sems):
    (slab_m, cg_m, rs_m, ag_m, ax_m, rhs_m, gs_m, ga_m, gx_m, ps_m, pa_m) = (
        sems[2 * i : 2 * i + 2] for i in range(11)
    )
    row, send_r, wait_r, drain_r, greet_r = helpers("row", nrow)
    col, send_c, wait_c, drain_c, greet_c = helpers("col", ncol)
    nb, _, cols = frames.shape
    rank = rf.shape[1]
    ch, pch = rank // nrow // share, cols // nrow
    mine = col if share > 1 else 0

    def gram_start(x, everything, got):
        gram = dot(x, x, ((0,), (0,)))
        for i in range(nrow * share):
            everything[i] = gram[i * ch : (i + 1) * ch]
        got[row] = everything[mine * nrow + row]

    def gram_scatter(everything, got, m):
        send_r(lambda p: everything.at[mine * nrow + p], got, m)

    def gram_gather(got, whole, m_in, m_out):
        wait_r(got, m_in)
        whole[mine, row] = total_of(got)
        send_r(lambda p: whole.at[mine, row], whole.at[mine], m_out)

    def gram_times(whole, other, m_in, m_x):
        wait_r(whole.at[mine], m_in)
        if share > 1:
            send_c(lambda p: whole.at[col], whole, m_x)
            wait_c(whole, m_x)
        for c in range(share):
            for i in range(nrow):
                at = (c * nrow + i) * ch
                mat[at : at + ch, :] = whole[c, i] * other[at : at + ch, :]

    def gram_drain(everything, got, whole, m_s, m_a, m_x):
        drain_r(lambda p: everything.at[mine * nrow + p], got, m_s)
        drain_r(lambda p: whole.at[mine, row], whole.at[mine], m_a)
        if share > 1:
            drain_c(lambda p: whole.at[col], whole, m_x)

    loads = [
        pltpu.make_async_copy(src, dst, in_s.at[i])
        for i, (src, dst) in enumerate(
            [(rf_h, rf), (cf_h, cf), (frames_h, frames), (tgram_h, tgram), (rhist_h, rhist), (chist_h, chist)]
        )
    ]
    for load in loads:
        load.start()
    greet_r()
    greet_c()
    loads[0].wait()
    gram_start(rf[...], gall, recv)
    loads[1].wait()
    cgram[col] = dot(cf[...], cf[...], ((0,), (0,)))
    pl.semaphore_wait(pltpu.get_barrier_semaphore(), nrow + ncol - 2)
    gram_scatter(gall, recv, rs_m)
    send_c(lambda p: cgram.at[col], cgram, cg_m)

    def slab_one(b, carry):
        slab[col, b] = dot(frames[b], cf[...], ((1,), (0,)))
        return carry

    loads[2].wait()
    lax.fori_loop(0, nb, slab_one, 0)
    gram_gather(recv, full, rs_m, ag_m)
    send_c(lambda p: slab.at[col], slab, slab_m)
    wait_c(cgram, cg_m)
    tnew[...] = total_of(cgram)
    wait_c(slab, slab_m)
    for b in range(nb):
        s = sum((slab[c, b] for c in range(1, ncol)), slab[0, b])
        total[b] = s
        rhs[row, b : b + 1, :] = jnp.sum(s * rf[...].astype(F32), axis=0, keepdims=True)
    rhs[row, nb:8, :] = jnp.zeros((8 - nb, rank), F32)
    gram_times(full, tnew, ag_m, ax_m)
    send_r(lambda p: rhs.at[row], rhs, rhs_m)
    factor(mat, below, w)
    wait_r(rhs, rhs_m)
    ff = solve(total_of(rhs), mat, below)
    o_f[...] = ff[:nb]

    for load in loads[3:]:
        load.wait()
    time_new = tgram[...] + dot(ff, ff, ((0,), (0,)), HIGHEST)
    mat[...] = time_new * tnew[...]
    tnew[...] = time_new
    factor(mat, below, w)
    sums = rhist[...]
    for b in range(nb):
        sums = sums + ff[b : b + 1, :] * total[b]
    new_row = solve(sums, mat, below).astype(jnp.bfloat16)
    o_row[...] = new_row

    gram_start(new_row, hall, hrecv)
    gram_scatter(hall, hrecv, gs_m)
    wide = 256

    def products(j):
        acc = jnp.zeros((wide, rank), F32)
        for b in range(nb):
            acc = acc + ff[b : b + 1, :] * dot(frames[b, :, j : j + wide], new_row, ((0,), (0,)))
        acc = acc.astype(jnp.bfloat16)
        for i in range(wide // pch):
            ppart[j // pch + i] = acc[i * pch : (i + 1) * pch]

    half = cols // 2
    for j in range(0, half, wide):
        products(j)
    gram_gather(hrecv, hfull, gs_m, ga_m)
    for j in range(half, cols, wide):
        products(j)
    gram_times(hfull, tnew, ga_m, gx_m)
    precv[row] = ppart[row]
    send_r(lambda p: ppart.at[p], precv, ps_m)
    factor(mat, below, w)
    wait_r(precv, ps_m)
    own = chist[pl.ds(pl.multiple_of(row * pch, pch), pch), :]
    for i in range(nrow):
        own = own + precv[i].astype(F32)
    pfull[row] = solve(own, mat, below).astype(jnp.bfloat16)

    inner = 4 if nrow % 4 == 0 else 1
    outer = nrow // inner
    group, place = row // inner, lax.rem(row, inner)

    def pass_on(chunk, to, sem):
        return pltpu.make_async_remote_copy(
            src_ref=pfull.at[chunk], dst_ref=pfull.at[chunk], send_sem=pa_m[0].at[sem],
            recv_sem=pa_m[1].at[chunk], device_id={"row": to}, device_id_type=MESH,
        )

    def across(d):
        return pass_on(row, lax.rem(group + d, outer) * inner + place, d)

    def within(d, e):
        chunk = lax.rem(group + outer - d, outer) * inner + place
        return pass_on(chunk, group * inner + lax.rem(place + e, inner), outer + d * inner + e)

    for d in range(1, outer):
        across(d).start()
    for d in range(outer):
        if d > 0:
            chunk = lax.rem(group + outer - d, outer) * inner + place
            pass_on(chunk, lax.rem(row + 1, nrow), 0).wait_recv()
        for e in range(1, inner):
            within(d, e).start()

    drain_c(lambda p: cgram.at[col], cgram, cg_m)
    drain_c(lambda p: slab.at[col], slab, slab_m)
    gram_drain(gall, recv, full, rs_m, ag_m, ax_m)
    drain_r(lambda p: rhs.at[row], rhs, rhs_m)
    gram_drain(hall, hrecv, hfull, gs_m, ga_m, gx_m)
    drain_r(lambda p: ppart.at[p], precv, ps_m)
    for d in range(outer):
        for e in range(1, inner):
            chunk = lax.rem(group + d, outer) * inner + lax.rem(place + e, inner)
            pass_on(chunk, lax.rem(row + 1, nrow), 0).wait_recv()
    for i in range(nrow):
        o_col[i * pch : (i + 1) * pch, :] = pfull[i]
    for d in range(outer):
        if d > 0:
            across(d).wait_send()
        for e in range(1, inner):
            within(d, e).wait_send()


def body(nrow, ncol, frames, rf, cf, rhist, chist, tgram):
    nb, rows, cols = frames.shape
    rank = rf.shape[1]
    share = ncol if rank % (8 * nrow * ncol) == 0 else 1
    ch, pch = rank // nrow // share, cols // nrow
    vm = pltpu.VMEM
    bf = jnp.bfloat16
    space = pl.BlockSpec(memory_space=vm)
    shape = jax.ShapeDtypeStruct
    counts = [ncol, ncol, nrow, nrow, ncol, nrow, nrow, nrow, ncol, nrow]
    square = vm((rank, rank), F32)
    quarter = vm((rank // 2, rank // 2), F32)
    part = vm((nrow, pch, rank), bf)
    gram = [
        vm((nrow * share, ch, rank), F32),
        vm((nrow, ch, rank), F32),
        vm((share, nrow, ch, rank), F32),
    ]
    return pl.pallas_call(
        functools.partial(kernel, nrow, ncol, share),
        out_shape=(shape((nb, rank), F32), shape((rows, rank), bf), shape((cols, rank), bf)),
        in_specs=[pl.BlockSpec(memory_space=pl.ANY)] * 6,
        out_specs=(space,) * 3,
        scratch_shapes=[vm(x.shape, x.dtype) for x in (frames, rf, cf, rhist, chist, tgram)] + [
            pltpu.SemaphoreType.DMA((6,)),
            vm((ncol, nb, rows, rank), F32), vm((ncol, rank, rank), F32), *gram, *gram,
            vm((nrow, 8, rank), F32), part, part, part,
            vm((nb, rows, rank), F32), square, quarter, quarter, square,
        ] + [pltpu.SemaphoreType.DMA((c,)) for c in counts for _ in range(2)]
        + [pltpu.SemaphoreType.DMA((2 * nrow + nrow // 4 + 1,)), pltpu.SemaphoreType.DMA((nrow,))],
        compiler_params=pltpu.CompilerParams(
            collective_id=0, has_side_effects=True, vmem_limit_bytes=VMEM_BYTES
        ),
    )(frames, rf, cf, rhist, chist, tgram)


def solution(mesh):
    in_specs = (
        P(None, "row", "col"),
        P("row", None),
        P("col", None),
        P("row", None),
        P("col", None),
        P(),
    )
    out_specs = (P(), P("row", None), P("col", None))
    return jax.shard_map(
        functools.partial(body, mesh.shape["row"], mesh.shape["col"]),
        mesh=mesh, in_specs=in_specs, out_specs=out_specs, check_vma=False,
    )
```

```python
import functools

import jax
import jax.numpy as jnp
from jax import lax
from jax.experimental import pallas as pl
from jax.experimental.pallas import tpu as pltpu
from jax.sharding import PartitionSpec as P

MESH = pl.DeviceIdType.MESH
HIGHEST = lax.Precision.HIGHEST
F32 = jnp.float32
VMEM_BYTES = 61 * 1024 * 1024
PIV = 8


def dot(a, b, dims, precision=None):
    return lax.dot_general(a, b, (dims, ((), ())), precision=precision, preferred_element_type=F32)


def reciprocal(x):
    r = pl.reciprocal(x, approx=True)
    for _ in range(2):
        r = r + r * (1.0 - x * r)
    return r


def eliminate(cols):
    cols = list(cols)
    sub = lax.broadcasted_iota(jnp.int32, cols[0].shape, 0)
    for k in range(PIV):
        row = [jnp.broadcast_to(c[k : k + 1, :], c.shape) for c in cols]
        p = reciprocal(row[k])
        ck = cols[k]
        here = sub == k
        for b in range(len(cols)):
            if b == k:
                cols[b] = jnp.where(here, p, -(ck * p))
            else:
                w = row[b] * p
                cols[b] = jnp.where(here, w, cols[b] - ck * w)
    return cols


def add_up(terms):
    while len(terms) > 1:
        terms = [sum(terms[i : i + 2][1:], terms[i]) for i in range(0, len(terms), 2)]
    return terms[0]


def invert(a_ref, w_ref):
    n = a_ref.shape[0]
    groups = n // PIV
    lane = lax.broadcasted_iota(jnp.int32, (PIV, n), 1)
    lanes = lax.broadcasted_iota(jnp.int32, (n, n), 1)

    def rows(g):
        return pl.ds(pl.multiple_of(g * PIV, PIV), PIV)

    def columns(tile, g):
        turned = pltpu.roll(tile, lax.rem(2 * n - g * PIV, n), 1)
        return [jnp.broadcast_to(turned[:, b : b + 1], (PIV, 128)) for b in range(PIV)]

    def wide(c):
        return jnp.concatenate([c] * (n // 128), axis=1) if n > 128 else c

    def times(cols, tile):
        return add_up([wide(cols[b]) * jnp.broadcast_to(tile[b : b + 1, :], (PIV, n)) for b in range(PIV)])

    def within(g, iota):
        return (iota >= g * PIV) & (iota < g * PIV + PIV)

    def update(tile, cols, w, g):
        return jnp.where(within(g, lane), 0.0, tile) - times(cols, w)

    def advance(g, tile, block, later):
        ahead = columns(later, g + 1)
        mult = columns(later, g)
        cols = eliminate(list(block) + columns(tile, g + 1))
        unit = (lane - g * PIV == lax.broadcasted_iota(jnp.int32, (PIV, n), 0)).astype(F32)
        w = times(cols[:PIV], jnp.where(within(g, lane), unit, tile))
        new_block = tuple(
            ahead[b] - add_up([mult[a] * jnp.broadcast_to(cols[PIV + b][a : a + 1, :], (PIV, 128)) for a in range(PIV)])
            for b in range(PIV)
        )
        return w, update(later, mult, w, g), new_block

    def bulk(g, w):
        w_ref[rows(g), :] = w
        inside = within(g, lanes)
        x = a_ref[...]
        a_ref[...] = jnp.where(inside, 0.0, x) - dot(
            jnp.where(inside, x, 0.0), w_ref[...], ((1,), (0,)), HIGHEST
        )
        a_ref[rows(g), :] = w
        w_ref[rows(g), :] = jnp.zeros_like(w)

    w_ref[...] = jnp.zeros_like(w_ref)
    tile = a_ref[0:PIV, :]
    carry = advance(0, tile, columns(tile, 0), a_ref[PIV : 2 * PIV, :])

    def group(g, carry):
        w, tile, block = carry
        later = a_ref[rows(lax.rem(g + 1, groups)), :]
        later = update(later, columns(later, g - 1), w, g - 1)
        out = advance(g, tile, block, later)
        bulk(g - 1, w)
        return out

    w = lax.fori_loop(1, groups, group, carry)[0]
    bulk(groups - 1, w)


def factor(mat, below, w):
    h = mat.shape[0] // 2
    top = mat.at[0:h, 0:h]
    rest = mat.at[h : 2 * h, h : 2 * h]
    invert(top, w)
    below[...] = dot(mat[h : 2 * h, 0:h], top[...], ((1,), (0,)), HIGHEST)
    rest[...] = rest[...] - dot(below[...], mat[0:h, h : 2 * h], ((1,), (0,)), HIGHEST)
    invert(rest, w)


def solve(rhs, mat, below):
    h = mat.shape[0] // 2
    one, two = rhs[:, 0:h], rhs[:, h : 2 * h]
    two = two - dot(one, below[...], ((1,), (1,)), HIGHEST)
    two = dot(two, mat[h : 2 * h, h : 2 * h], ((1,), (0,)), HIGHEST)
    one = dot(one, mat[0:h, 0:h], ((1,), (0,)), HIGHEST) - dot(two, below[...], ((1,), (0,)), HIGHEST)
    return jnp.concatenate([one, two], axis=1)


def helpers(axis, count):
    me = lax.axis_index(axis)

    def each(fn):
        def one(d, carry):
            fn(lax.rem(me + d, count))
            return carry
        lax.fori_loop(1, count, one, 0)

    def copy(p, src, buf, sems, slot):
        return pltpu.make_async_remote_copy(
            src_ref=src, dst_ref=buf.at[slot], send_sem=sems[0].at[p], recv_sem=sems[1].at[slot],
            device_id={axis: p}, device_id_type=MESH,
        )

    def send(src, buf, sems):
        each(lambda p: copy(p, src(p), buf, sems, me).start())

    def wait(buf, sems):
        each(lambda p: copy(p, buf.at[p], buf, sems, p).wait_recv())

    def drain(src, buf, sems):
        each(lambda p: copy(p, src(p), buf, sems, me).wait_send())

    def greet():
        each(lambda p: pl.semaphore_signal(
            pltpu.get_barrier_semaphore(), inc=1, device_id={axis: p}, device_id_type=MESH))

    return me, send, wait, drain, greet


def total_of(ref):
    return sum((ref[i] for i in range(1, ref.shape[0])), ref[0])


def kernel(nrow, ncol, share, frames_h, rf_h, cf_h, rhist_h, chist_h, tgram_h,
           o_f, o_row, o_col, frames, rf, cf, rhist, chist, tgram, in_s, slab, cgram, gall, recv, full, hall, hrecv, hfull, rhs, ppart, precv, pfull,
           total, mat, w, below, tnew, *sems):
    (slab_m, cg_m, rs_m, ag_m, ax_m, rhs_m, gs_m, ga_m, gx_m, ps_m, pa_m) = (
        sems[2 * i : 2 * i + 2] for i in range(11)
    )
    row, send_r, wait_r, drain_r, greet_r = helpers("row", nrow)
    col, send_c, wait_c, drain_c, greet_c = helpers("col", ncol)
    nb, _, cols = frames.shape
    rank = rf.shape[1]
    ch, pch = rank // nrow // share, cols // nrow
    mine = col if share > 1 else 0

    def gram_start(x, everything, got):
        gram = dot(x, x, ((0,), (0,)))
        for i in range(nrow * share):
            everything[i] = gram[i * ch : (i + 1) * ch]
        got[row] = everything[mine * nrow + row]

    def gram_scatter(everything, got, m):
        send_r(lambda p: everything.at[mine * nrow + p], got, m)

    def gram_gather(got, whole, m_in, m_out):
        wait_r(got, m_in)
        whole[mine, row] = total_of(got)
        send_r(lambda p: whole.at[mine, row], whole.at[mine], m_out)

    def gram_times(whole, other, m_in, m_x):
        wait_r(whole.at[mine], m_in)
        if share > 1:
            send_c(lambda p: whole.at[col], whole, m_x)
            wait_c(whole, m_x)
        for c in range(share):
            for i in range(nrow):
                at = (c * nrow + i) * ch
                mat[at : at + ch, :] = whole[c, i] * other[at : at + ch, :]

    def gram_drain(everything, got, whole, m_s, m_a, m_x):
        drain_r(lambda p: everything.at[mine * nrow + p], got, m_s)
        drain_r(lambda p: whole.at[mine, row], whole.at[mine], m_a)
        if share > 1:
            drain_c(lambda p: whole.at[col], whole, m_x)

    loads = [
        pltpu.make_async_copy(src, dst, in_s.at[i])
        for i, (src, dst) in enumerate(
            [(rf_h, rf), (cf_h, cf), (frames_h, frames), (tgram_h, tgram), (rhist_h, rhist), (chist_h, chist)]
        )
    ]
    for load in loads:
        load.start()
    greet_r()
    greet_c()
    loads[0].wait()
    gram_start(rf[...], gall, recv)
    loads[1].wait()
    cgram[col] = dot(cf[...], cf[...], ((0,), (0,)))
    pl.semaphore_wait(pltpu.get_barrier_semaphore(), nrow + ncol - 2)
    gram_scatter(gall, recv, rs_m)
    send_c(lambda p: cgram.at[col], cgram, cg_m)

    def slab_one(b, carry):
        slab[col, b] = dot(frames[b], cf[...], ((1,), (0,)))
        return carry

    loads[2].wait()
    lax.fori_loop(0, nb, slab_one, 0)
    gram_gather(recv, full, rs_m, ag_m)
    send_c(lambda p: slab.at[col], slab, slab_m)
    wait_c(cgram, cg_m)
    tnew[...] = total_of(cgram)
    wait_c(slab, slab_m)
    for b in range(nb):
        s = sum((slab[c, b] for c in range(1, ncol)), slab[0, b])
        total[b] = s
        rhs[row, b : b + 1, :] = jnp.sum(s * rf[...].astype(F32), axis=0, keepdims=True)
    rhs[row, nb:8, :] = jnp.zeros((8 - nb, rank), F32)
    gram_times(full, tnew, ag_m, ax_m)
    send_r(lambda p: rhs.at[row], rhs, rhs_m)
    factor(mat, below, w)
    wait_r(rhs, rhs_m)
    ff = solve(total_of(rhs), mat, below)
    o_f[...] = ff[:nb]

    for load in loads[3:]:
        load.wait()
    time_new = tgram[...] + dot(ff, ff, ((0,), (0,)), HIGHEST)
    mat[...] = time_new * tnew[...]
    tnew[...] = time_new
    factor(mat, below, w)
    sums = rhist[...]
    for b in range(nb):
        sums = sums + ff[b : b + 1, :] * total[b]
    new_row = solve(sums, mat, below).astype(jnp.bfloat16)
    o_row[...] = new_row

    gram_start(new_row, hall, hrecv)
    gram_scatter(hall, hrecv, gs_m)
    wide = 256

    def products(j):
        acc = jnp.zeros((wide, rank), F32)
        for b in range(nb):
            acc = acc + ff[b : b + 1, :] * dot(frames[b, :, j : j + wide], new_row, ((0,), (0,)))
        acc = acc.astype(jnp.bfloat16)
        for i in range(wide // pch):
            ppart[j // pch + i] = acc[i * pch : (i + 1) * pch]

    half = cols // 2
    for j in range(0, half, wide):
        products(j)
    gram_gather(hrecv, hfull, gs_m, ga_m)
    for j in range(half, cols, wide):
        products(j)
    gram_times(hfull, tnew, ga_m, gx_m)
    precv[row] = ppart[row]
    send_r(lambda p: ppart.at[p], precv, ps_m)
    factor(mat, below, w)
    wait_r(precv, ps_m)
    own = chist[pl.ds(pl.multiple_of(row * pch, pch), pch), :]
    for i in range(nrow):
        own = own + precv[i].astype(F32)
    pfull[row] = solve(own, mat, below).astype(jnp.bfloat16)

    inner = 4 if nrow % 4 == 0 else 1
    outer = nrow // inner
    group, place = row // inner, lax.rem(row, inner)

    def pass_on(chunk, to, sem):
        return pltpu.make_async_remote_copy(
            src_ref=pfull.at[chunk], dst_ref=pfull.at[chunk], send_sem=pa_m[0].at[sem],
            recv_sem=pa_m[1].at[chunk], device_id={"row": to}, device_id_type=MESH,
        )

    def across(d):
        return pass_on(row, lax.rem(group + d, outer) * inner + place, d)

    def within(d, e):
        chunk = lax.rem(group + outer - d, outer) * inner + place
        return pass_on(chunk, group * inner + lax.rem(place + e, inner), outer + d * inner + e)

    for d in range(1, outer):
        across(d).start()
    for d in range(outer):
        if d > 0:
            chunk = lax.rem(group + outer - d, outer) * inner + place
            pass_on(chunk, lax.rem(row + 1, nrow), 0).wait_recv()
        for e in range(1, inner):
            within(d, e).start()

    drain_c(lambda p: cgram.at[col], cgram, cg_m)
    drain_c(lambda p: slab.at[col], slab, slab_m)
    gram_drain(gall, recv, full, rs_m, ag_m, ax_m)
    drain_r(lambda p: rhs.at[row], rhs, rhs_m)
    gram_drain(hall, hrecv, hfull, gs_m, ga_m, gx_m)
    drain_r(lambda p: ppart.at[p], precv, ps_m)
    for d in range(outer):
        for e in range(1, inner):
            chunk = lax.rem(group + d, outer) * inner + lax.rem(place + e, inner)
            pass_on(chunk, lax.rem(row + 1, nrow), 0).wait_recv()
    for i in range(nrow):
        o_col[i * pch : (i + 1) * pch, :] = pfull[i]
    for d in range(outer):
        if d > 0:
            across(d).wait_send()
        for e in range(1, inner):
            within(d, e).wait_send()


def body(nrow, ncol, frames, rf, cf, rhist, chist, tgram):
    nb, rows, cols = frames.shape
    rank = rf.shape[1]
    share = ncol if rank % (8 * nrow * ncol) == 0 else 1
    ch, pch = rank // nrow // share, cols // nrow
    vm = pltpu.VMEM
    bf = jnp.bfloat16
    space = pl.BlockSpec(memory_space=vm)
    shape = jax.ShapeDtypeStruct
    counts = [ncol, ncol, nrow, nrow, ncol, nrow, nrow, nrow, ncol, nrow]
    square = vm((rank, rank), F32)
    quarter = vm((rank // 2, rank // 2), F32)
    part = vm((nrow, pch, rank), bf)
    gram = [
        vm((nrow * share, ch, rank), F32),
        vm((nrow, ch, rank), F32),
        vm((share, nrow, ch, rank), F32),
    ]
    return pl.pallas_call(
        functools.partial(kernel, nrow, ncol, share),
        out_shape=(shape((nb, rank), F32), shape((rows, rank), bf), shape((cols, rank), bf)),
        in_specs=[pl.BlockSpec(memory_space=pl.ANY)] * 6,
        out_specs=(space,) * 3,
        scratch_shapes=[vm(x.shape, x.dtype) for x in (frames, rf, cf, rhist, chist, tgram)] + [
            pltpu.SemaphoreType.DMA((6,)),
            vm((ncol, nb, rows, rank), F32), vm((ncol, rank, rank), F32), *gram, *gram,
            vm((nrow, 8, rank), F32), part, part, part,
            vm((nb, rows, rank), F32), square, quarter, quarter, square,
        ] + [pltpu.SemaphoreType.DMA((c,)) for c in counts for _ in range(2)]
        + [pltpu.SemaphoreType.DMA((2 * nrow + nrow // 4 + 1,)), pltpu.SemaphoreType.DMA((nrow,))],
        compiler_params=pltpu.CompilerParams(
            collective_id=0, has_side_effects=True, vmem_limit_bytes=VMEM_BYTES
        ),
    )(frames, rf, cf, rhist, chist, tgram)


def solution(mesh):
    in_specs = (
        P(None, "row", "col"),
        P("row", None),
        P("col", None),
        P("row", None),
        P("col", None),
        P(),
    )
    out_specs = (P(), P("row", None), P("col", None))
    return jax.shard_map(
        functools.partial(body, mesh.shape["row"], mesh.shape["col"]),
        mesh=mesh, in_specs=in_specs, out_specs=out_specs, check_vma=False,
    )
```
